256 devices in a mesh: member: 16 (over y, x_lo, core), space: 16 (over x_hi, z).
Axes of the slice: x: 4 (x_hi: 2, x_lo: 2; x = x_hi * 2 + x_lo), y: 4, z: 8, core: 2. Of those that a mesh axis runs over, the one named last changes fastest.
Arguments:
- layer_input: bfloat16 [64, 4096, 256], P('member', 'space'), may hold values from -6 to 6
- out_grad: bfloat16 [64, 4096, 256], P('member', 'space'), may hold values from -6 to 6
- norm1_gain: float32 [256], replicated, as said below
- w_query: bfloat16 [256, 256], replicated, as said below
- w_key: bfloat16 [256, 256], replicated, as said below
- w_value: bfloat16 [256, 256], replicated, may hold values from -0.375 to 0.375
- w_out: bfloat16 [256, 256], replicated, may hold values from -0.375 to 0.375
- norm2_gain: float32 [256], replicated, may hold values from 0.5 to 1.5
- w_up: bfloat16 [256, 1024], replicated, may hold values from -0.375 to 0.375
- w_down: bfloat16 [1024, 256], replicated, may hold values from -0.1875 to 0.1875
Outputs:
- input_grad: float32 [64, 4096, 256], P('member', 'space')
- grad_query: float32 [256, 256], replicated
- grad_key: float32 [256, 256], replicated
- grad_value: float32 [256, 256], replicated
- grad_wout: float32 [256, 256], replicated
- grad_up: float32 [256, 1024], replicated
- grad_down: float32 [1024, 256], replicated
- grad_gain1: float32 [256], replicated
- grad_gain2: float32 [256], replicated
The draws below stay inside these ranges and needn't reach their ends.
Inputs may be any that keep to these rules, and one draw needn't show every extreme that they name: `norm1_gain`: positive gains, between 0.5 and 3. `w_query`: entries of a query projection. `w_key`: entries of a key projection.
All inputs are finite; a program needn't handle non-finite values.
Results may differ from the reference program's by a relative error of at most 0.008.
The reference program's roundings to bfloat16 on the way count: a program that leaves them out, or rounds other values in their place, can miss the bound.
Values may be sent and summed in bfloat16 or wider, within the bound.
No kernel may reach another device: no remote copies, remote signals or barrier semaphores. Data moves between devices by JAX's collectives and lax.ppermute only.
A program may use at most 128 MiB of HBM per device.

```python
import math
import jax
import jax.numpy as jnp
from jax import lax

D = 256
HEAD_DIM = 32
FF = 1024
MEMBERS = 64
PATCHES = 4096


def shared_rows(key):
    base = jax.random.truncated_normal(jax.random.fold_in(key, 101), -3.0, 3.0, (D, D), jnp.float32) * D ** (-0.5)
    return base


def draw_w_query(key, part):
    base = shared_rows(key)
    return base.astype(jnp.bfloat16)


def draw_w_key(key, part):
    key = jax.random.fold_in(key, 7)
    own = jax.random.truncated_normal(key, -3.0, 3.0, (D, D), jnp.float32) * D ** (-0.5)
    return own.astype(jnp.bfloat16)


def draw_norm1_gain(key, part):
    key = jax.random.fold_in(key, 3)
    return jax.random.uniform(key, (D,), jnp.float32, 0.5, 1.5)


def block_levels(stream_key, shape, cuts, least, largest):
    def one(axis_at, blocks):
        heights = jax.random.uniform(jax.random.fold_in(jax.random.fold_in(stream_key, 6), axis_at), (blocks,), jnp.float32, least / len(cuts), largest / len(cuts))
        return jnp.repeat(jnp.exp(heights), shape[axis_at] // blocks).reshape((-1,) + (1,) * (len(shape) - axis_at - 1))

    level = one(*cuts[0])
    for cut in cuts[1:]:
        level = level * one(*cut)
    return level


def centred(rng, extent, spread, limit, cuts=(), held_as=jnp.bfloat16):
    gain = block_levels(rng, extent, cuts, -0.22, 0.18) if cuts else 1.0
    values = jax.random.normal(rng, extent, jnp.float32) * spread * gain
    return jnp.minimum(jnp.maximum(values, -limit), limit).astype(held_as)


def setup_inputs(seed: int = 0) -> dict:
    key_of = jax.random.split(jax.random.key(seed), 11)
    layer_input = centred(key_of[0], (MEMBERS, PATCHES, D), 1.0, 6.0, ((0, 16), (1, 16)))
    out_grad = centred(key_of[1], (MEMBERS, PATCHES, D), 1.0, 6.0, ((0, 16), (1, 16)))
    norm1_gain = draw_norm1_gain(jax.random.fold_in(key_of[10], 71), 0)
    w_query = draw_w_query(jax.random.fold_in(key_of[10], 71), 0)
    w_key = draw_w_key(jax.random.fold_in(key_of[10], 71), 0)
    w_value = centred(key_of[5], (D, D), D ** -0.5, 0.375)
    w_out = centred(key_of[6], (D, D), D ** -0.5, 0.375)
    norm2_gain = jnp.clip(1.0 + 0.1 * jax.random.normal(key_of[7], (D,), jnp.float32), 0.5, 1.5)
    w_up = centred(key_of[8], (D, FF), D ** -0.5, 0.375)
    w_down = centred(key_of[9], (FF, D), FF ** -0.5, 0.1875)
    return {"layer_input": layer_input, "out_grad": out_grad, "norm1_gain": norm1_gain, "w_query": w_query, "w_key": w_key, "w_value": w_value, "w_out": w_out, "norm2_gain": norm2_gain, "w_up": w_up, "w_down": w_down}


EPS = 1e-06
GELU_C = 0.7978845608028654
GELU_A = 0.044715

def multiply(form, left, right):
    return jnp.einsum(form, left.astype(jnp.float32), right.astype(jnp.float32))

def norm_rows(values):
    inverse = lax.rsqrt(lax.optimization_barrier(jnp.mean(values * values, axis=-1, keepdims=True)) + EPS)
    return (values * inverse, inverse)

def norm_back(unit_rows, inverse, gains, upstream):
    scaled = upstream * gains
    into = inverse * (scaled - unit_rows * lax.optimization_barrier(jnp.mean(scaled * unit_rows, axis=-1, keepdims=True)))
    return (into, lax.optimization_barrier(jnp.sum(upstream * unit_rows, axis=(0, 1))))

def gelu_pair(preact):
    tangent = jnp.tanh(GELU_C * (preact + GELU_A * preact * preact * preact))
    result = 0.5 * preact * (1.0 + tangent)
    slopes = 0.5 * (1.0 + tangent) + 0.5 * preact * (1.0 - tangent * tangent) * GELU_C * (1.0 + 3.0 * GELU_A * preact * preact)
    return (result, slopes)

def attend(query, keys, values, heads):
    members, count, width = query.shape
    shape_four = (members, count, heads, width // heads)
    scale = 1.0 / math.sqrt(width // heads)
    scores = multiply('mphe,nphe->phmn', query.reshape(shape_four), keys.reshape(shape_four)) * scale
    scores = scores - lax.optimization_barrier(jnp.max(scores, axis=-1, keepdims=True))
    weights = jnp.exp(scores)
    weights = weights / lax.optimization_barrier(jnp.sum(weights, axis=-1, keepdims=True))
    rounded = weights.astype(jnp.bfloat16)
    mixed = multiply('phmn,nphe->mphe', rounded, values.reshape(shape_four)).astype(jnp.bfloat16)
    return (weights, rounded, mixed.reshape(members, count, width))

def attend_back(query, keys, values, weights, rounded, upstream, heads):
    members, count, width = query.shape
    shape_four = (members, count, heads, width // heads)
    scale = 1.0 / math.sqrt(width // heads)
    up_four = upstream.reshape(shape_four)
    dprob = multiply('mphe,nphe->phmn', up_four, values.reshape(shape_four))
    grad_v = multiply('phmn,mphe->nphe', rounded, up_four).astype(jnp.bfloat16)
    dscore = (weights * (dprob - lax.optimization_barrier(jnp.sum(weights * dprob, axis=-1, keepdims=True))) * scale).astype(jnp.bfloat16)
    grad_q = multiply('phmn,nphe->mphe', dscore, keys.reshape(shape_four)).astype(jnp.bfloat16)
    grad_k = multiply('phmn,mphe->nphe', dscore, query.reshape(shape_four)).astype(jnp.bfloat16)
    return (grad_q.reshape(members, count, width), grad_k.reshape(members, count, width), grad_v.reshape(members, count, width))

def layer_block(inputs, cotangent, norm1_gain, w_query, w_key, w_value, w_out, norm2_gain, w_up, w_down):
    heads = inputs.shape[-1] // HEAD_DIM
    wide = inputs.astype(jnp.float32)
    unit1, inverse1 = norm_rows(wide)
    normed1 = (unit1 * norm1_gain).astype(jnp.bfloat16)
    query = multiply('mpd,de->mpe', normed1, w_query).astype(jnp.bfloat16)
    keys = multiply('mpd,de->mpe', normed1, w_key).astype(jnp.bfloat16)
    values = multiply('mpd,de->mpe', normed1, w_value).astype(jnp.bfloat16)
    weights, rounded, mixed = attend(query, keys, values, heads)
    hidden_state = wide + multiply('mpd,de->mpe', mixed, w_out)
    unit2, inverse2 = norm_rows(hidden_state)
    normed2 = (unit2 * norm2_gain).astype(jnp.bfloat16)
    preact = multiply('mpd,df->mpf', normed2, w_up)
    activated, slopes = gelu_pair(preact)
    activated = activated.astype(jnp.bfloat16)
    part_down = multiply('mpf,mpd->fd', activated, cotangent)
    grad_act = multiply('mpd,fd->mpf', cotangent, w_down)
    grad_pre = (grad_act * slopes).astype(jnp.bfloat16)
    part_up = multiply('mpd,mpf->df', normed2, grad_pre)
    grad_normed2 = multiply('mpf,df->mpd', grad_pre, w_up)
    back_two, part_gain2 = norm_back(unit2, inverse2, norm2_gain, grad_normed2)
    grad_hidden = cotangent.astype(jnp.float32) + back_two
    grad_attn = grad_hidden.astype(jnp.bfloat16)
    part_wout = multiply('mpd,mpe->de', mixed, grad_attn)
    grad_mixed = multiply('mpe,de->mpd', grad_attn, w_out).astype(jnp.bfloat16)
    grad_q, grad_k, grad_v = attend_back(query, keys, values, weights, rounded, grad_mixed, heads)
    part_query = multiply('mpd,mpe->de', normed1, grad_q)
    part_key = multiply('mpd,mpe->de', normed1, grad_k)
    part_value = multiply('mpd,mpe->de', normed1, grad_v)
    grad_normed1 = multiply('mpe,de->mpd', grad_q, w_query) + multiply('mpe,de->mpd', grad_k, w_key) + multiply('mpe,de->mpd', grad_v, w_value)
    back_one, part_gain1 = norm_back(unit1, inverse1, norm1_gain, grad_normed1)
    input_grad = grad_hidden + back_one
    return (input_grad, (part_query, part_key, part_value, part_wout, part_up, part_down, part_gain1, part_gain2))

def reference(layer_input, out_grad, norm1_gain, w_query, w_key, w_value, w_out, norm2_gain, w_up, w_down):
    block_size = math.gcd(PATCHES, 64)
    block_count = PATCHES // block_size

    def split_blocks(array):
        return array.reshape(MEMBERS, block_count, block_size, D).transpose(1, 0, 2, 3)
    square = jnp.zeros((D, D), jnp.float32)
    starting = (square, square, square, square, jnp.zeros((D, FF), jnp.float32), jnp.zeros((FF, D), jnp.float32), jnp.zeros((D,), jnp.float32), jnp.zeros((D,), jnp.float32))

    def advance(running, blocks):
        grad_in, parts = layer_block(blocks[0], blocks[1], norm1_gain, w_query, w_key, w_value, w_out, norm2_gain, w_up, w_down)
        return (tuple((first + second for first, second in zip(running, parts))), grad_in)
    totals, pieces = lax.scan(advance, starting, (split_blocks(layer_input), split_blocks(out_grad)))
    input_grad = pieces.transpose(1, 0, 2, 3).reshape(MEMBERS, PATCHES, D)
    scale = 1.0 / math.sqrt(MEMBERS * PATCHES)
    scaled = [part * scale for part in totals]
    return (input_grad, scaled[0], scaled[1], scaled[2], scaled[3], scaled[4], scaled[5], scaled[6], scaled[7])
```

```python
import math

import jax
import jax.numpy as jnp
from jax import lax
from jax.sharding import PartitionSpec as P

HEAD_DIM = 32


EPS = 1e-06
GELU_C = 0.7978845608028654
GELU_A = 0.044715


def multiply(form, left, right):
    return jnp.einsum(form, left, right, preferred_element_type=jnp.float32)


def norm_rows(values):
    inverse = lax.rsqrt(jnp.mean(values * values, axis=-1, keepdims=True) + EPS)
    return (values * inverse, inverse)


def norm_back(unit_rows, inverse, gains, upstream):
    scaled = upstream * gains
    into = inverse * (scaled - unit_rows * jnp.mean(scaled * unit_rows, axis=-1, keepdims=True))
    return (into, jnp.sum(upstream * unit_rows, axis=(0, 1)))


def gelu_pair(preact):
    tangent = jnp.tanh(GELU_C * (preact + GELU_A * preact * preact * preact))
    result = 0.5 * preact * (1.0 + tangent)
    slopes = 0.5 * (1.0 + tangent) + 0.5 * preact * (1.0 - tangent * tangent) * GELU_C * (
        1.0 + 3.0 * GELU_A * preact * preact
    )
    return (result, slopes)


def attend(query, keys, values, heads):
    members, count, width = query.shape
    shape_four = (members, count, heads, width // heads)
    scale = 1.0 / math.sqrt(width // heads)
    scores = (
        multiply("mphe,nphe->phmn", query.reshape(shape_four), keys.reshape(shape_four)) * scale
    )
    scores = scores - jnp.max(scores, axis=-1, keepdims=True)
    weights = jnp.exp(scores)
    weights = weights / jnp.sum(weights, axis=-1, keepdims=True)
    rounded = weights.astype(jnp.bfloat16)
    mixed = multiply("phmn,nphe->mphe", rounded, values.reshape(shape_four)).astype(jnp.bfloat16)
    return (weights, rounded, mixed.reshape(members, count, width))


def attend_back(query, keys, values, weights, rounded, upstream, heads):
    members, count, width = query.shape
    shape_four = (members, count, heads, width // heads)
    scale = 1.0 / math.sqrt(width // heads)
    up_four = upstream.reshape(shape_four)
    dprob = multiply("mphe,nphe->phmn", up_four, values.reshape(shape_four))
    grad_v = multiply("phmn,mphe->nphe", rounded, up_four).astype(jnp.bfloat16)
    dscore = (weights * (dprob - jnp.sum(weights * dprob, axis=-1, keepdims=True)) * scale).astype(
        jnp.bfloat16
    )
    grad_q = multiply("phmn,nphe->mphe", dscore, keys.reshape(shape_four)).astype(jnp.bfloat16)
    grad_k = multiply("phmn,mphe->nphe", dscore, query.reshape(shape_four)).astype(jnp.bfloat16)
    return (
        grad_q.reshape(members, count, width),
        grad_k.reshape(members, count, width),
        grad_v.reshape(members, count, width),
    )


def layer(
    layer_input, out_grad, norm1_gain, w_query, w_key, w_value, w_out, norm2_gain, w_up, w_down
):
    heads = layer_input.shape[-1] // HEAD_DIM
    wide = layer_input.astype(jnp.float32)
    unit1, inverse1 = norm_rows(wide)
    normed1 = (unit1 * norm1_gain).astype(jnp.bfloat16)
    query = multiply("mpd,de->mpe", normed1, w_query).astype(jnp.bfloat16)
    keys = multiply("mpd,de->mpe", normed1, w_key).astype(jnp.bfloat16)
    values = multiply("mpd,de->mpe", normed1, w_value).astype(jnp.bfloat16)
    weights, rounded, mixed = attend(query, keys, values, heads)
    hidden_state = wide + multiply("mpd,de->mpe", mixed, w_out)
    unit2, inverse2 = norm_rows(hidden_state)
    normed2 = (unit2 * norm2_gain).astype(jnp.bfloat16)
    preact = multiply("mpd,df->mpf", normed2, w_up)
    activated, slopes = gelu_pair(preact)
    activated = activated.astype(jnp.bfloat16)
    part_down = multiply("mpf,mpd->fd", activated, out_grad)
    grad_act = multiply("mpd,fd->mpf", out_grad, w_down)
    grad_pre = (grad_act * slopes).astype(jnp.bfloat16)
    part_up = multiply("mpd,mpf->df", normed2, grad_pre)
    grad_normed2 = multiply("mpf,df->mpd", grad_pre, w_up)
    back_two, part_gain2 = norm_back(unit2, inverse2, norm2_gain, grad_normed2)
    grad_hidden = out_grad.astype(jnp.float32) + back_two
    grad_attn = grad_hidden.astype(jnp.bfloat16)
    part_wout = multiply("mpd,mpe->de", mixed, grad_attn)
    grad_mixed = multiply("mpe,de->mpd", grad_attn, w_out).astype(jnp.bfloat16)
    grad_q, grad_k, grad_v = attend_back(query, keys, values, weights, rounded, grad_mixed, heads)
    part_query = multiply("mpd,mpe->de", normed1, grad_q)
    part_key = multiply("mpd,mpe->de", normed1, grad_k)
    part_value = multiply("mpd,mpe->de", normed1, grad_v)
    grad_normed1 = (
        multiply("mpe,de->mpd", grad_q, w_query)
        + multiply("mpe,de->mpd", grad_k, w_key)
        + multiply("mpe,de->mpd", grad_v, w_value)
    )
    back_one, part_gain1 = norm_back(unit1, inverse1, norm1_gain, grad_normed1)
    moved = (back_two + back_one).astype(jnp.bfloat16)
    up_blocks = part_up.reshape(256, 4, 256).transpose(1, 0, 2).reshape(1024, 256)
    weights_all = jnp.concatenate(
        [part_query, part_key, part_value, part_wout, up_blocks, part_down], axis=0
    ).astype(jnp.bfloat16)
    gains = jnp.stack([part_gain1, part_gain2])
    return moved, weights_all, gains


def two_parts(values):
    high = values.astype(jnp.bfloat16)
    low = (values - high.astype(jnp.float32)).astype(jnp.bfloat16)
    return jnp.concatenate([high, low], axis=0)


def swap(array, axis, groups=None):
    return lax.all_to_all(
        array, axis, split_axis=0, concat_axis=0, tiled=True, axis_index_groups=groups
    )


def add_everywhere(weights_all, gains):
    f32, b16 = jnp.float32, jnp.bfloat16
    members = lax.axis_size("member")
    spaces = lax.axis_size("space")
    chips = members // 2
    core = lax.axis_index("member") % 2
    other_core = [(k, k ^ 1) for k in range(members)]
    same_core = [[c + 2 * k for k in range(chips)] for c in range(2)]
    rows = weights_all.shape[0]

    def gain_rows(values):
        return jnp.concatenate([two_parts(values), jnp.zeros((4, 256), b16)], axis=0)

    halves = weights_all.reshape(2, rows // 2, 256)
    keep = lax.dynamic_index_in_dim(halves, core, 0, keepdims=False)
    give = lax.dynamic_index_in_dim(halves, 1 - core, 0, keepdims=False)
    sent = jnp.concatenate([give, gain_rows(gains)], axis=0)
    got = lax.ppermute(sent, "member", other_core)
    total = keep.astype(f32) + got[: rows // 2].astype(f32)
    gains = gains + got[rows // 2 : rows // 2 + 2].astype(f32) + got[rows // 2 + 2 : rows // 2 + 4].astype(f32)

    each = rows // 2 // chips
    sent = jnp.concatenate(
        [
            total.astype(b16).reshape(chips, each, 256),
            jnp.broadcast_to(gain_rows(gains), (chips, 8, 256)),
        ],
        axis=1,
    )
    got = swap(sent, "member", same_core).astype(f32).sum(axis=0)
    total = got[:each]
    gains = got[each : each + 2] + got[each + 2 : each + 4]

    small = each * 2 // spaces
    sent = jnp.concatenate(
        [
            total.astype(b16).reshape(spaces, small, 128),
            jnp.broadcast_to(two_parts(gains.reshape(4, 128)), (spaces, 8, 128)),
        ],
        axis=1,
    )
    got = swap(sent, "space").astype(f32).sum(axis=0)
    total = got[:small].astype(b16)
    gains = (got[small : small + 4] + got[small + 4 : small + 8]).reshape(2, 256)

    everywhere = swap(jnp.broadcast_to(total, (spaces, small, 128)), "space")
    everywhere = everywhere.reshape(each, 256)
    everywhere = swap(jnp.broadcast_to(everywhere, (chips, each, 256)), "member", same_core)
    mine = everywhere.reshape(rows // 2, 256)
    theirs = lax.ppermute(mine, "member", other_core)
    first = jnp.where(core == 0, mine, theirs)
    second = jnp.where(core == 0, theirs, mine)
    return jnp.concatenate([first, second], axis=0).astype(f32), gains


def on_device(
    layer_input, out_grad, norm1_gain, w_query, w_key, w_value, w_out, norm2_gain, w_up, w_down
):
    groups = lax.axis_size("member")
    own_members, own_patches, width = layer_input.shape
    spread = own_patches // groups
    everyone = own_members * groups

    def patchwise(array):
        return array.reshape(own_members, groups, spread, width).transpose(1, 0, 2, 3)

    both = jnp.concatenate([patchwise(layer_input), patchwise(out_grad)], axis=1)
    both = swap(both, "member")
    inputs_here = both[:, :own_members].reshape(everyone, spread, width)
    out_grad_here = both[:, own_members:].reshape(everyone, spread, width)
    moved, weights_all, gains = layer(
        inputs_here, out_grad_here, norm1_gain, w_query, w_key, w_value, w_out, norm2_gain, w_up, w_down
    )
    home = swap(moved.reshape(groups, own_members, spread, width), "member")
    home = home.transpose(1, 0, 2, 3).reshape(own_members, own_patches, width)
    input_grad = out_grad.astype(jnp.float32) + home.astype(jnp.float32)
    totals, gains = add_everywhere(weights_all, gains)
    scale = 1.0 / math.sqrt(everyone * own_patches * lax.axis_size("space"))
    totals = totals * scale
    gains = gains * scale
    return (
        input_grad,
        totals[0:256],
        totals[256:512],
        totals[512:768],
        totals[768:1024],
        totals[1024:2048].reshape(4, 256, 256).transpose(1, 0, 2).reshape(256, 1024),
        totals[2048:3072],
        gains[0],
        gains[1],
    )


def solution(mesh):
    in_specs = (
        P("member", "space", None),
        P("member", "space", None),
        P(),
        P(),
        P(),
        P(),
        P(),
        P(),
        P(),
        P(),
    )
    out_specs = (P("member", "space", None), P(), P(), P(), P(), P(), P(), P(), P())
    return jax.shard_map(
        on_device, mesh=mesh, in_specs=in_specs, out_specs=out_specs, check_vma=False
    )
```

```python
import functools
import math

import jax
import jax.numpy as jnp
from jax import lax
from jax.experimental import pallas as pl
from jax.experimental.pallas import tpu as pltpu
from jax.sharding import PartitionSpec as P

HEAD_DIM = 32
WIDTH = 256
HIDDEN = 1024
HEADS = WIDTH // HEAD_DIM
GROUPS = 16
CHIPS = 8
OWN = 4
SPREAD = 16
MEMBERS = GROUPS * OWN
TOKENS = MEMBERS * SPREAD
PIECE = OWN * SPREAD
LANES = HEADS * MEMBERS
BLOCK = 256
PER_BLOCK = BLOCK // MEMBERS
ROWS = 192
GAIN_ROWS = 8
CHUNK = ROWS + GAIN_ROWS
SLAB = 24
SMALL = SLAB + GAIN_ROWS

EPS = 1e-06
GELU_C = 0.7978845608028654
GELU_A = 0.044715
SCALE = 1.0 / math.sqrt(HEAD_DIM)

F32 = jnp.float32
B16 = jnp.bfloat16
VMEM = pl.BlockSpec(memory_space=pltpu.VMEM)
SMEM = pl.BlockSpec(memory_space=pltpu.SMEM)


def dot(left, right, contract):
    return lax.dot_general(left, right, ((contract[:1], contract[1:]), ((), ())), preferred_element_type=F32)


def norm_rows(values):
    inverse = lax.rsqrt(jnp.mean(values * values, axis=-1, keepdims=True) + EPS)
    return values * inverse, inverse


def norm_back(unit_rows, inverse, gains, upstream):
    scaled = upstream * gains
    return inverse * (scaled - unit_rows * jnp.mean(scaled * unit_rows, axis=-1, keepdims=True))


def gelu_pair(preact):
    square = preact * preact
    tangent = jnp.tanh(GELU_C * (preact + GELU_A * preact * square))
    half = 0.5 * (1.0 + tangent)
    slopes = half + 0.5 * preact * (1.0 - tangent * tangent) * (
        GELU_C * (1.0 + 3.0 * GELU_A * square)
    )
    return preact * half, slopes


def own_heads(stacked):
    lane_head = lax.broadcasted_iota(jnp.int32, (MEMBERS, WIDTH), 1) // HEAD_DIM
    result = stacked[:MEMBERS]
    for head in range(1, HEADS):
        result = jnp.where(lane_head == head, stacked[head * MEMBERS : (head + 1) * MEMBERS], result)
    return result


def layer_kernel(
    core_ref,
    both_ref,
    gain1_ref,
    wqkv_ref,
    wout_ref,
    gain2_ref,
    wup_ref,
    wdown_ref,
    keep_ref,
    give_ref,
    xs,
    gs,
    ds,
    mask,
    qkv,
    expanded,
    probs,
    rounded,
    mixs,
    gmix,
    n1s,
    n2s,
    gas,
    ogs,
    gqkv,
    gpre,
    acts,
    gain_sums,
    parts,
):
    core = core_ref[0]
    for group in range(GROUPS):
        rows = slice(group * PIECE, (group + 1) * PIECE)
        for side in range(2):
            lanes = slice(side * 128, (side + 1) * 128)
            xs[side, rows] = both_ref[group, :PIECE, lanes].astype(F32)
            gs[side, rows] = both_ref[group, PIECE:, lanes].astype(F32)
    mask[...] = (
        lax.broadcasted_iota(jnp.int32, (LANES, WIDTH), 0) // MEMBERS
        == lax.broadcasted_iota(jnp.int32, (LANES, WIDTH), 1) // HEAD_DIM
    ).astype(F32).astype(B16)
    gain_sums[...] = jnp.zeros_like(gain_sums)
    gain1 = gain1_ref[...]
    gain2 = gain2_ref[...]

    def block(step, carry):
        base = pl.multiple_of(step * BLOCK, BLOCK)
        here = pl.ds(base, BLOCK)

        def patches(ref):
            return jnp.concatenate(
                [
                    jnp.concatenate(
                        [ref[side, pl.ds(step * PER_BLOCK + j, MEMBERS, stride=SPREAD), :] for j in range(PER_BLOCK)],
                        axis=0,
                    )
                    for side in range(2)
                ],
                axis=1,
            )

        wide = patches(xs)
        unit1, inverse1 = norm_rows(wide)
        normed1 = (unit1 * gain1).astype(B16)
        n1s[here] = normed1
        qkv[...] = jnp.dot(normed1, wqkv_ref[...], preferred_element_type=F32).astype(B16)
        for j in range(PER_BLOCK):
            rows = slice(j * MEMBERS, (j + 1) * MEMBERS)
            query, keys, values = (qkv[rows, i * WIDTH : (i + 1) * WIDTH] for i in range(3))
            spread_query = jnp.concatenate([query] * HEADS, axis=0) * mask[...]
            expanded[j] = spread_query
            scores = dot(keys, spread_query, (1, 1)) * SCALE
            scores = jnp.exp(scores - jnp.max(scores, axis=0, keepdims=True))
            weights = scores * (1.0 / jnp.sum(scores, axis=0, keepdims=True))
            probs[j] = weights
            narrow = weights.astype(B16)
            rounded[j] = narrow
            mixs[pl.ds(base + j * MEMBERS, MEMBERS)] = own_heads(dot(narrow, values, (0, 0))).astype(B16)

        cotangent = patches(gs)
        cotangent_narrow = cotangent.astype(B16)
        ogs[here] = cotangent_narrow
        hidden = wide + jnp.dot(mixs[here], wout_ref[...], preferred_element_type=F32)
        unit2, inverse2 = norm_rows(hidden)
        normed2 = (unit2 * gain2).astype(B16)
        n2s[here] = normed2
        activated, slopes = gelu_pair(jnp.dot(normed2, wup_ref[...], preferred_element_type=F32))
        acts[here] = activated.astype(B16)
        grad_pre = (dot(cotangent_narrow, wdown_ref[...], (1, 1)) * slopes).astype(B16)
        gpre[here] = grad_pre
        grad_normed2 = dot(grad_pre, wup_ref[...], (1, 1))
        gain_sums[1:2] += jnp.sum(grad_normed2 * unit2, axis=0, keepdims=True)
        back_two = norm_back(unit2, inverse2, gain2, grad_normed2)
        grad_attn = (cotangent + back_two).astype(B16)
        gas[here] = grad_attn
        gmix[...] = dot(grad_attn, wout_ref[...], (1, 1)).astype(B16)
        for j in range(PER_BLOCK):
            rows = slice(j * MEMBERS, (j + 1) * MEMBERS)
            there = pl.ds(base + j * MEMBERS, MEMBERS)
            keys, values = (qkv[rows, i * WIDTH : (i + 1) * WIDTH] for i in (1, 2))
            spread_grad = jnp.concatenate([gmix[rows]] * HEADS, axis=0) * mask[...]
            dprob = dot(values, spread_grad, (1, 1))
            grad_v = jnp.dot(rounded[j], spread_grad, preferred_element_type=F32)
            weights = probs[j]
            product = weights * dprob
            dscore = (
                (product - weights * jnp.sum(product, axis=0, keepdims=True)) * SCALE
            ).astype(B16)
            grad_k = jnp.dot(dscore, expanded[j], preferred_element_type=F32)
            grad_q = own_heads(dot(dscore, keys, (0, 0)))
            gqkv[there, :WIDTH] = grad_q.astype(B16)
            gqkv[there, WIDTH : 2 * WIDTH] = grad_k.astype(B16)
            gqkv[there, 2 * WIDTH :] = grad_v.astype(B16)
        grad_normed1 = dot(gqkv[here], wqkv_ref[...], (1, 1))
        gain_sums[0:1] += jnp.sum(grad_normed1 * unit1, axis=0, keepdims=True)
        delta = back_two + norm_back(unit1, inverse1, gain1, grad_normed1)
        for j in range(PER_BLOCK):
            for side in range(2):
                ds[side, pl.ds(step * PER_BLOCK + j, MEMBERS, stride=SPREAD), :] = delta[
                    j * MEMBERS : (j + 1) * MEMBERS, side * 128 : (side + 1) * 128
                ]
        return carry

    lax.fori_loop(0, TOKENS // BLOCK, block, 0)

    part_qkv = dot(n1s[...], gqkv[...], (0, 0)).astype(B16)
    for i in range(3):
        parts[i * WIDTH : (i + 1) * WIDTH] = part_qkv[:, i * WIDTH : (i + 1) * WIDTH]
    parts[3 * WIDTH : 4 * WIDTH] = dot(mixs[...], gas[...], (0, 0)).astype(B16)
    part_up = dot(n2s[...], gpre[...], (0, 0)).astype(B16)
    for i in range(4):
        parts[(4 + i) * WIDTH : (5 + i) * WIDTH] = part_up[:, i * WIDTH : (i + 1) * WIDTH]
    part_down = dot(ogs[...], acts[...], (0, 0))
    for i in range(4):
        parts[(8 + i) * WIDTH : (9 + i) * WIDTH] = part_down[:, i * WIDTH : (i + 1) * WIDTH].T.astype(B16)
    gain_rows = gain_sums[...].astype(B16)
    for target, side in ((keep_ref, core), (give_ref, 1 - core)):
        for chip in range(CHIPS):
            start = pl.multiple_of(side * (CHIPS * ROWS) + chip * ROWS, ROWS)
            target[chip, :ROWS] = parts[pl.ds(start, ROWS)]
            target[chip, ROWS:CHUNK] = gain_rows
            start = pl.multiple_of((2 * chip + side) * PIECE, PIECE)
            for lane in range(2):
                target[chip, CHUNK:, lane * 128 : (lane + 1) * 128] = ds[lane, pl.ds(start, PIECE)].astype(B16)


def run_layer(core, both, gain1, wqkv, wout, gain2, wup, wdown):
    scratch = [
        pltpu.VMEM((2, TOKENS, 128), F32),
        pltpu.VMEM((2, TOKENS, 128), F32),
        pltpu.VMEM((2, TOKENS, 128), F32),
        pltpu.VMEM((LANES, WIDTH), B16),
        pltpu.VMEM((BLOCK, 3 * WIDTH), B16),
        pltpu.VMEM((PER_BLOCK, LANES, WIDTH), B16),
        pltpu.VMEM((PER_BLOCK, MEMBERS, LANES), F32),
        pltpu.VMEM((PER_BLOCK, MEMBERS, LANES), B16),
        pltpu.VMEM((TOKENS, WIDTH), B16),
        pltpu.VMEM((BLOCK, WIDTH), B16),
        pltpu.VMEM((TOKENS, WIDTH), B16),
        pltpu.VMEM((TOKENS, WIDTH), B16),
        pltpu.VMEM((TOKENS, WIDTH), B16),
        pltpu.VMEM((TOKENS, WIDTH), B16),
        pltpu.VMEM((TOKENS, 3 * WIDTH), B16),
        pltpu.VMEM((TOKENS, HIDDEN), B16),
        pltpu.VMEM((TOKENS, HIDDEN), B16),
        pltpu.VMEM((GAIN_ROWS, WIDTH), F32),
        pltpu.VMEM((2 * CHIPS * ROWS, WIDTH), B16),
    ]
    shape = jax.ShapeDtypeStruct((CHIPS, CHUNK + PIECE, WIDTH), B16)
    return pl.pallas_call(
        layer_kernel,
        out_shape=(shape, shape),
        in_specs=[SMEM] + [VMEM] * 7,
        out_specs=(VMEM, VMEM),
        scratch_shapes=scratch,
        compiler_params=pltpu.CompilerParams(vmem_limit_bytes=48 * 1024 * 1024),
        cost_estimate=pl.CostEstimate(flops=5_000_000_000, bytes_accessed=6_000_000, transcendentals=2_000_000),
    )(core, both, gain1, wqkv, wout, gain2, wup, wdown)


def pack_kernel(input_ref, grad_ref, out_ref):
    for group in range(GROUPS):
        for own in range(OWN):
            there = slice(group * SPREAD, (group + 1) * SPREAD)
            out_ref[group, own * SPREAD : (own + 1) * SPREAD] = input_ref[own, there]
            out_ref[group, PIECE + own * SPREAD : PIECE + (own + 1) * SPREAD] = grad_ref[own, there]


def pair_kernel(keep_ref, got_ref, out_ref):
    for chip in range(CHIPS):
        total = keep_ref[chip, :CHUNK].astype(F32) + got_ref[chip, :CHUNK].astype(F32)
        out_ref[chip, :CHUNK] = total.astype(B16)
        out_ref[chip, CHUNK : CHUNK + PIECE] = keep_ref[chip, CHUNK:]
        out_ref[chip, CHUNK + PIECE :] = got_ref[chip, CHUNK:]


def sum_kernel(got_ref, out_ref):
    total = got_ref[0, :CHUNK].astype(F32)
    for chip in range(1, CHIPS):
        total = total + got_ref[chip, :CHUNK].astype(F32)
    for slab in range(CHIPS):
        for side in range(2):
            lanes = slice(side * 128, (side + 1) * 128)
            out_ref[2 * slab + side, :SLAB] = total[slab * SLAB : (slab + 1) * SLAB, lanes].astype(B16)
            out_ref[2 * slab + side, SLAB:] = total[ROWS:, lanes].astype(B16)


def home_kernel(core_ref, got_ref, grad_ref, out_ref):
    core = core_ref[0]
    for chip in range(CHIPS):
        for part in range(2):
            index = 2 * chip + (core if part == 0 else 1 - core)
            there = pl.ds(pl.multiple_of(index * SPREAD, SPREAD), SPREAD)
            first = CHUNK + part * PIECE
            for own in range(OWN):
                moved = got_ref[chip, first + own * SPREAD : first + (own + 1) * SPREAD]
                out_ref[own, there] = grad_ref[own, there].astype(F32) + moved.astype(F32)


def spread_kernel(got_ref, out_ref, gains_ref):
    for slab in range(CHIPS):
        for side in range(2):
            lanes = slice(side * 128, (side + 1) * 128)
            piece = got_ref[2 * slab + side, :SLAB]
            for chip in range(CHIPS):
                out_ref[chip, slab * SLAB : (slab + 1) * SLAB, lanes] = piece
    for side in range(2):
        gains_ref[:, side * 128 : (side + 1) * 128] = got_ref[side, SLAB:]


def final_kernel(
    scale, core_ref, mine_ref, theirs_ref, gains_ref, q_ref, k_ref, v_ref, o_ref, up_ref, down_ref, g1_ref, g2_ref
):
    core = core_ref[0]

    def fill(low_ref, high_ref):
        def low(index):
            return low_ref[index * WIDTH : (index + 1) * WIDTH].astype(F32) * scale

        def high(index):
            return high_ref[index * WIDTH : (index + 1) * WIDTH].astype(F32) * scale

        for index, ref in enumerate((q_ref, k_ref, v_ref, o_ref)):
            ref[...] = low(index)
        for index in range(2):
            up_ref[:, index * WIDTH : (index + 1) * WIDTH] = low(4 + index)
            up_ref[:, (2 + index) * WIDTH : (3 + index) * WIDTH] = high(index)
        for index in range(4):
            down_ref[index * WIDTH : (index + 1) * WIDTH] = high(2 + index)

    @pl.when(core == 0)
    def _():
        fill(mine_ref, theirs_ref)

    @pl.when(core != 0)
    def _():
        fill(theirs_ref, mine_ref)

    gains = gains_ref[...].astype(F32) * scale
    g1_ref[...] = gains[0:1]
    g2_ref[...] = gains[1:2]


def local(kernel, out_shape, specs, *operands):
    return pl.pallas_call(
        kernel,
        out_shape=out_shape,
        in_specs=specs,
        out_specs=jax.tree.map(lambda _: VMEM, out_shape),
        compiler_params=pltpu.CompilerParams(vmem_limit_bytes=32 * 1024 * 1024),
    )(*operands)


def shaped(*shape, dtype=B16):
    return jax.ShapeDtypeStruct(shape, dtype)


def swap(array, axis, groups=None):
    return lax.all_to_all(
        array, axis, split_axis=0, concat_axis=0, tiled=True, axis_index_groups=groups
    )


def on_device(
    layer_input, out_grad, norm1_gain, w_query, w_key, w_value, w_out, norm2_gain, w_up, w_down
):
    members = lax.axis_size("member")
    spaces = lax.axis_size("space")
    core = (lax.axis_index("member") % 2).astype(jnp.int32).reshape(1)
    other_core = [(k, k ^ 1) for k in range(members)]
    same_core = [[c + 2 * k for k in range(CHIPS)] for c in range(2)]

    both = local(pack_kernel, shaped(GROUPS, 2 * PIECE, WIDTH), [VMEM] * 2, layer_input, out_grad)
    both = swap(both, "member")
    wqkv = jnp.concatenate([w_query, w_key, w_value], axis=1)
    keep, give = run_layer(
        core, both, norm1_gain.reshape(1, WIDTH), wqkv, w_out, norm2_gain.reshape(1, WIDTH), w_up, w_down
    )
    got = lax.ppermute(give, "member", other_core)
    sent = local(pair_kernel, shaped(CHIPS, CHUNK + 2 * PIECE, WIDTH), [VMEM] * 2, keep, got)
    got = swap(sent, "member", same_core)
    input_grad = local(
        home_kernel, shaped(OWN, GROUPS * SPREAD, WIDTH, dtype=F32), [SMEM, VMEM, VMEM], core, got, out_grad
    )
    sent = local(sum_kernel, shaped(spaces, SMALL, 128), [VMEM], got)
    total = swap(sent, "space").astype(F32).sum(axis=0).astype(B16)
    everywhere = swap(jnp.broadcast_to(total, (spaces, SMALL, 128)), "space")
    sent, gains = local(
        spread_kernel, (shaped(CHIPS, ROWS, WIDTH), shaped(GAIN_ROWS, WIDTH)), [VMEM], everywhere
    )
    mine = swap(sent, "member", same_core).reshape(CHIPS * ROWS, WIDTH)
    theirs = lax.ppermute(mine, "member", other_core)
    scale = 1.0 / math.sqrt(MEMBERS * GROUPS * SPREAD * spaces)
    square = shaped(WIDTH, WIDTH, dtype=F32)
    row = shaped(1, WIDTH, dtype=F32)
    grads = local(
        functools.partial(final_kernel, scale),
        (square, square, square, square, shaped(WIDTH, HIDDEN, dtype=F32), shaped(HIDDEN, WIDTH, dtype=F32), row, row),
        [SMEM, VMEM, VMEM, VMEM],
        core,
        mine,
        theirs,
        gains,
    )
    return (input_grad, *grads[:6], grads[6].reshape(WIDTH), grads[7].reshape(WIDTH))


def solution(mesh):
    in_specs = (
        P("member", "space", None),
        P("member", "space", None),
        P(),
        P(),
        P(),
        P(),
        P(),
        P(),
        P(),
        P(),
    )
    out_specs = (P("member", "space", None), P(), P(), P(), P(), P(), P(), P(), P())
    return jax.shard_map(
        on_device, mesh=mesh, in_specs=in_specs, out_specs=out_specs, check_vma=False
    )
```

```python
import functools
import math

import jax
import jax.numpy as jnp
from jax import lax
from jax.experimental import pallas as pl
from jax.experimental.pallas import tpu as pltpu
from jax.sharding import PartitionSpec as P

HEAD_DIM = 32
WIDTH = 256
HIDDEN = 1024
HEADS = WIDTH // HEAD_DIM
GROUPS = 16
CHIPS = 8
OWN = 4
SPREAD = 16
MEMBERS = GROUPS * OWN
TOKENS = MEMBERS * SPREAD
PIECE = OWN * SPREAD
HALF = WIDTH // 2
HALF_HEADS = HEADS // 2
LANES = HALF_HEADS * MEMBERS
ROWS = 192
GAIN_ROWS = 8
CHUNK = ROWS + GAIN_ROWS
SLAB = 24
SMALL = SLAB + GAIN_ROWS

EPS = 1e-06
GELU_C = 0.7978845608028654
GELU_A = 0.044715
SCALE = 1.0 / math.sqrt(HEAD_DIM)

F32 = jnp.float32
B16 = jnp.bfloat16
VMEM = pl.BlockSpec(memory_space=pltpu.VMEM)
ANY = pl.BlockSpec(memory_space=pl.ANY)
SMEM = pl.BlockSpec(memory_space=pltpu.SMEM)


def dot(left, right, contract):
    return lax.dot_general(left, right, ((contract[:1], contract[1:]), ((), ())), preferred_element_type=F32)


def norm_rows(values):
    inverse = lax.rsqrt(jnp.mean(values * values, axis=-1, keepdims=True) + EPS)
    return values * inverse, inverse


def norm_back(unit_rows, inverse, gains, upstream):
    scaled = upstream * gains
    return inverse * (scaled - unit_rows * jnp.mean(scaled * unit_rows, axis=-1, keepdims=True))


def gelu_pair(preact):
    square = preact * preact
    half = 0.5 + 0.5 * jnp.tanh(preact * (GELU_C + (GELU_C * GELU_A) * square))
    bend = preact * (2.0 * GELU_C + (6.0 * GELU_C * GELU_A) * square)
    return preact * half, half + (half - half * half) * bend


def own_heads(stacked):
    lane_head = lax.broadcasted_iota(jnp.int32, (MEMBERS, HALF), 1) // HEAD_DIM
    result = stacked[:MEMBERS]
    for head in range(1, HALF_HEADS):
        result = jnp.where(lane_head == head, stacked[head * MEMBERS : (head + 1) * MEMBERS], result)
    return result


def layer_kernel(
    core_ref,
    both_ref,
    gain1_ref,
    wqkv_ref,
    wout_ref,
    gain2_ref,
    wup_ref,
    wdown_ref,
    keep_ref,
    give_ref,
    xs,
    gs,
    ds,
    mask,
    qkv,
    expanded,
    probs,
    dprobs,
    rounded,
    mixs,
    gmix,
    n1s,
    n2s,
    gas,
    ogs,
    gqkv,
    gpre,
    acts,
    unit1s,
    unit2s,
    backs,
    products,
    wide_products,
    parts,
):
    core = core_ref[0]
    halves = [slice(side * HALF, (side + 1) * HALF) for side in range(2)]
    blocks = [slice(patch * MEMBERS, (patch + 1) * MEMBERS) for patch in range(SPREAD)]
    for group in range(GROUPS):
        rows = slice(group * PIECE, (group + 1) * PIECE)
        for side, lanes in enumerate(halves):
            xs[side, rows] = both_ref[group, 0, :, :, lanes].astype(F32).reshape(PIECE, HALF)
            gs[side, rows] = both_ref[group, 1, :, :, lanes].astype(F32).reshape(PIECE, HALF)
    mask[...] = (
        lax.broadcasted_iota(jnp.int32, (LANES, HALF), 0) // MEMBERS
        == lax.broadcasted_iota(jnp.int32, (LANES, HALF), 1) // HEAD_DIM
    ).astype(F32).astype(B16)
    gain1 = gain1_ref[...]
    gain2 = gain2_ref[...]

    def patch_rows(ref, patch):
        return jnp.concatenate(
            [ref[side, pl.ds(patch, MEMBERS, stride=SPREAD), :] for side in range(2)], axis=1
        )

    def spread_heads(rows):
        return jnp.concatenate([rows] * HALF_HEADS, axis=0) * mask[...]

    inverse1 = []
    for patch, rows in enumerate(blocks):
        unit, inverse = norm_rows(patch_rows(xs, patch))
        unit1s[rows] = unit
        inverse1.append(inverse)
        n1s[rows] = (unit * gain1).astype(B16)
        ogs[rows] = patch_rows(gs, patch).astype(B16)
    for i in range(3):
        lanes = slice(i * WIDTH, (i + 1) * WIDTH)
        qkv[:, lanes] = jnp.dot(n1s[...], wqkv_ref[:, lanes], preferred_element_type=F32).astype(B16)

    units = [(patch, side) for patch in range(SPREAD) for side in range(2)]

    def part(ref, index, patch, side):
        return ref[blocks[patch], index * WIDTH + side * HALF : index * WIDTH + (side + 1) * HALF]

    def staged(stages):
        lag = 4
        for step in range(0, len(units) + lag * (len(stages) - 1), lag):
            for late, stage in enumerate(stages):
                for unit in units[max(step - lag * late, 0) : max(step - lag * late + lag, 0)]:
                    stage(*unit)

    def score(patch, side):
        spread_query = spread_heads(part(qkv, 0, patch, side))
        expanded[patch, side] = spread_query
        probs[patch, side] = dot(part(qkv, 1, patch, side), spread_query, (1, 1)) * SCALE

    def soften(patch, side):
        scores = probs[patch, side]
        scores = jnp.exp(scores - jnp.max(scores, axis=0, keepdims=True))
        weights = scores * (1.0 / jnp.sum(scores, axis=0, keepdims=True))
        probs[patch, side] = weights
        rounded[patch, side] = weights.astype(B16)

    def mix(patch, side):
        mixed = own_heads(dot(rounded[patch, side], part(qkv, 2, patch, side), (0, 0)))
        mixs[blocks[patch], halves[side]] = mixed.astype(B16)

    staged((score, soften, mix))
    products[...] = jnp.dot(mixs[...], wout_ref[...], preferred_element_type=F32)
    inverse2 = []
    for patch, rows in enumerate(blocks):
        unit, inverse = norm_rows(patch_rows(xs, patch) + products[rows])
        unit2s[rows] = unit
        inverse2.append(inverse)
        n2s[rows] = (unit * gain2).astype(B16)

    for i in range(HIDDEN // WIDTH):
        lanes = slice(i * WIDTH, (i + 1) * WIDTH)
        wide_products[i % 2, 0] = jnp.dot(n2s[...], wup_ref[:, lanes], preferred_element_type=F32)
        wide_products[i % 2, 1] = dot(ogs[...], wdown_ref[lanes], (1, 1))
        for rows in blocks:
            activated, slopes = gelu_pair(wide_products[i % 2, 0, rows])
            acts[rows, lanes] = activated.astype(B16)
            gpre[rows, lanes] = (wide_products[i % 2, 1, rows] * slopes).astype(B16)
    products[...] = dot(gpre[...], wup_ref[...], (1, 1))
    gain2_sum = jnp.zeros((MEMBERS, WIDTH), F32)
    for patch, rows in enumerate(blocks):
        unit, grad = unit2s[rows], products[rows]
        gain2_sum = gain2_sum + grad * unit
        back = norm_back(unit, inverse2[patch], gain2, grad)
        backs[rows] = back
        gas[rows] = (ogs[rows].astype(F32) + back).astype(B16)
    gmix[...] = dot(gas[...], wout_ref[...], (1, 1)).astype(B16)

    def keep_grad(index, patch, side, grad):
        gqkv[blocks[patch], index * WIDTH + side * HALF : index * WIDTH + (side + 1) * HALF] = grad.astype(B16)

    def meet(patch, side):
        spread_grad = spread_heads(gmix[blocks[patch], halves[side]])
        dprobs[patch, side] = dot(part(qkv, 2, patch, side), spread_grad, (1, 1))
        keep_grad(2, patch, side, jnp.dot(rounded[patch, side], spread_grad, preferred_element_type=F32))

    def bend(patch, side):
        weights = probs[patch, side]
        product = weights * dprobs[patch, side]
        dscore = (product - weights * jnp.sum(product, axis=0, keepdims=True)) * SCALE
        rounded[patch, side] = dscore.astype(B16)

    def finish(patch, side):
        dscore = rounded[patch, side]
        keep_grad(1, patch, side, jnp.dot(dscore, expanded[patch, side], preferred_element_type=F32))
        keep_grad(0, patch, side, own_heads(dot(dscore, part(qkv, 1, patch, side), (0, 0))))

    staged((meet, bend, finish))
    products[...] = dot(gqkv[...], wqkv_ref[...], (1, 1))
    gain1_sum = jnp.zeros((MEMBERS, WIDTH), F32)
    for patch, rows in enumerate(blocks):
        unit, grad = unit1s[rows], products[rows]
        gain1_sum = gain1_sum + grad * unit
        delta = backs[rows] + norm_back(unit, inverse1[patch], gain1, grad)
        for side, lanes in enumerate(halves):
            ds[side, pl.ds(patch, MEMBERS, stride=SPREAD), :] = delta[:, lanes]

    for i in range(3):
        parts[i * WIDTH : (i + 1) * WIDTH] = dot(
            n1s[...], gqkv[:, i * WIDTH : (i + 1) * WIDTH], (0, 0)
        ).astype(B16)
    parts[3 * WIDTH : 4 * WIDTH] = dot(mixs[...], gas[...], (0, 0)).astype(B16)
    for i in range(4):
        parts[(4 + i) * WIDTH : (5 + i) * WIDTH] = dot(
            n2s[...], gpre[:, i * WIDTH : (i + 1) * WIDTH], (0, 0)
        ).astype(B16)
    for i in range(4):
        part_down = dot(ogs[...], acts[:, i * WIDTH : (i + 1) * WIDTH], (0, 0))
        parts[(8 + i) * WIDTH : (9 + i) * WIDTH] = part_down.T.astype(B16)
    gain_rows = jnp.concatenate(
        [jnp.sum(total, axis=0, keepdims=True) for total in (gain1_sum, gain2_sum)]
        + [jnp.zeros((GAIN_ROWS - 2, WIDTH), F32)],
        axis=0,
    ).astype(B16)
    for target, side in ((keep_ref, core), (give_ref, 1 - core)):
        for chip in range(CHIPS):
            start = pl.multiple_of(side * (CHIPS * ROWS) + chip * ROWS, ROWS)
            target[chip, :ROWS] = parts[pl.ds(start, ROWS)]
            target[chip, ROWS:CHUNK] = gain_rows
            start = pl.multiple_of((2 * chip + side) * PIECE, PIECE)
            for half, lanes in enumerate(halves):
                target[chip, CHUNK:, lanes] = ds[half, pl.ds(start, PIECE)].astype(B16)


def run_layer(core, both, gain1, wqkv, wout, gain2, wup, wdown):
    rows = (TOKENS, WIDTH)
    scratch = [
        pltpu.VMEM((2, TOKENS, HALF), F32),
        pltpu.VMEM((2, TOKENS, HALF), F32),
        pltpu.VMEM((2, TOKENS, HALF), F32),
        pltpu.VMEM((LANES, HALF), B16),
        pltpu.VMEM((TOKENS, 3 * WIDTH), B16),
        pltpu.VMEM((SPREAD, 2, LANES, HALF), B16),
        pltpu.VMEM((SPREAD, 2, MEMBERS, LANES), F32),
        pltpu.VMEM((SPREAD, 2, MEMBERS, LANES), F32),
        pltpu.VMEM((SPREAD, 2, MEMBERS, LANES), B16),
        pltpu.VMEM(rows, B16),
        pltpu.VMEM(rows, B16),
        pltpu.VMEM(rows, B16),
        pltpu.VMEM(rows, B16),
        pltpu.VMEM(rows, B16),
        pltpu.VMEM(rows, B16),
        pltpu.VMEM((TOKENS, 3 * WIDTH), B16),
        pltpu.VMEM((TOKENS, HIDDEN), B16),
        pltpu.VMEM((TOKENS, HIDDEN), B16),
        pltpu.VMEM(rows, F32),
        pltpu.VMEM(rows, F32),
        pltpu.VMEM(rows, F32),
        pltpu.VMEM(rows, F32),
        pltpu.VMEM((2, 2, *rows), F32),
        pltpu.VMEM((2 * CHIPS * ROWS, WIDTH), B16),
    ]
    shape = shaped(CHIPS, CHUNK + PIECE, WIDTH)
    return pl.pallas_call(
        layer_kernel,
        out_shape=(shape, shape),
        in_specs=[SMEM] + [VMEM] * 7,
        out_specs=(VMEM, VMEM),
        scratch_shapes=scratch,
        compiler_params=pltpu.CompilerParams(vmem_limit_bytes=48 * 1024 * 1024),
        cost_estimate=pl.CostEstimate(flops=5_000_000_000, bytes_accessed=6_000_000, transcendentals=2_000_000),
    )(core, both, gain1, wqkv, wout, gain2, wup, wdown)


def pack_kernel(input_ref, grad_ref, out_ref, sems):
    copies = []
    for group in range(GROUPS):
        there = slice(group * SPREAD, (group + 1) * SPREAD)
        for side, ref in enumerate((input_ref, grad_ref)):
            copies.append(
                pltpu.make_async_copy(ref.at[:, there], out_ref.at[group, side], sems.at[group, side])
            )
    for copy in copies:
        copy.start()
    for copy in copies:
        copy.wait()


def pack(layer_input, out_grad):
    return pl.pallas_call(
        pack_kernel,
        out_shape=shaped(GROUPS, 2, OWN, SPREAD, WIDTH),
        in_specs=[ANY, ANY],
        out_specs=VMEM,
        scratch_shapes=[pltpu.SemaphoreType.DMA((GROUPS, 2))],
    )(layer_input, out_grad)


def pair_kernel(keep_ref, got_ref, out_ref):
    for chip in range(CHIPS):
        total = keep_ref[chip, :CHUNK].astype(F32) + got_ref[chip, :CHUNK].astype(F32)
        out_ref[chip, :CHUNK] = total.astype(B16)
        out_ref[chip, CHUNK : CHUNK + PIECE] = keep_ref[chip, CHUNK:]
        out_ref[chip, CHUNK + PIECE :] = got_ref[chip, CHUNK:]


def sum_kernel(got_ref, out_ref):
    total = got_ref[0, :CHUNK].astype(F32)
    for chip in range(1, CHIPS):
        total = total + got_ref[chip, :CHUNK].astype(F32)
    out_ref[...] = total.astype(B16)


def four(refs):
    own, first, second, third = (ref[...].astype(F32) for ref in refs)
    return ((own + first) + (second + third)).astype(B16)


def round_kernel(own_ref, first_ref, second_ref, third_ref, out_ref):
    out_ref[...] = four((own_ref, first_ref, second_ref, third_ref))


def last_round_kernel(own_ref, first_ref, second_ref, third_ref, out_ref, gains_ref):
    total = four((own_ref, first_ref, second_ref, third_ref))
    for chip in range(CHIPS):
        out_ref[chip] = total[:ROWS]
    gains_ref[...] = total[ROWS:]


def home_kernel(core_ref, got_ref, grad_ref, out_ref):
    core = core_ref[0]
    for chip in range(CHIPS):
        for part in range(2):
            index = 2 * chip + (core if part == 0 else 1 - core)
            there = pl.ds(pl.multiple_of(index * SPREAD, SPREAD), SPREAD)
            first = CHUNK + part * PIECE
            for own in range(OWN):
                moved = got_ref[chip, first + own * SPREAD : first + (own + 1) * SPREAD]
                out_ref[own, there] = grad_ref[own, there].astype(F32) + moved.astype(F32)


def final_kernel(
    scale, core_ref, mine_ref, theirs_ref, gains_ref, q_ref, k_ref, v_ref, o_ref, up_ref, down_ref, g1_ref, g2_ref
):
    core = core_ref[0]

    def fill(low_ref, high_ref):
        def low(index):
            return low_ref[index * WIDTH : (index + 1) * WIDTH].astype(F32) * scale

        def high(index):
            return high_ref[index * WIDTH : (index + 1) * WIDTH].astype(F32) * scale

        for index, ref in enumerate((q_ref, k_ref, v_ref, o_ref)):
            ref[...] = low(index)
        for index in range(2):
            up_ref[:, index * WIDTH : (index + 1) * WIDTH] = low(4 + index)
            up_ref[:, (2 + index) * WIDTH : (3 + index) * WIDTH] = high(index)
        for index in range(4):
            down_ref[index * WIDTH : (index + 1) * WIDTH] = high(2 + index)

    @pl.when(core == 0)
    def _():
        fill(mine_ref, theirs_ref)

    @pl.when(core != 0)
    def _():
        fill(theirs_ref, mine_ref)

    gains = gains_ref[...].astype(F32) * scale
    g1_ref[...] = gains[0:1]
    g2_ref[...] = gains[1:2]


def local(kernel, out_shape, specs, *operands):
    return pl.pallas_call(
        kernel,
        out_shape=out_shape,
        in_specs=specs,
        out_specs=jax.tree.map(lambda _: VMEM, out_shape),
        compiler_params=pltpu.CompilerParams(vmem_limit_bytes=32 * 1024 * 1024),
    )(*operands)


def shaped(*shape, dtype=B16):
    return jax.ShapeDtypeStruct(shape, dtype)


def swap(array, axis, groups=None):
    return lax.all_to_all(
        array, axis, split_axis=0, concat_axis=0, tiled=True, axis_index_groups=groups
    )


def on_device(
    layer_input, out_grad, norm1_gain, w_query, w_key, w_value, w_out, norm2_gain, w_up, w_down
):
    members = lax.axis_size("member")
    spaces = lax.axis_size("space")
    core = (lax.axis_index("member") % 2).astype(jnp.int32).reshape(1)
    other_core = [(k, k ^ 1) for k in range(members)]
    same_core = [[c + 2 * k for k in range(CHIPS)] for c in range(2)]

    def across(array, steps):
        return [lax.ppermute(array, "space", [(k, k ^ step) for k in range(spaces)]) for step in steps]

    both = swap(pack(layer_input, out_grad), "member")
    wqkv = jnp.concatenate([w_query, w_key, w_value], axis=1)
    keep, give = run_layer(
        core, both, norm1_gain.reshape(1, WIDTH), wqkv, w_out, norm2_gain.reshape(1, WIDTH), w_up, w_down
    )
    got = lax.ppermute(give, "member", other_core)
    sent = local(pair_kernel, shaped(CHIPS, CHUNK + 2 * PIECE, WIDTH), [VMEM] * 2, keep, got)
    got = swap(sent, "member", same_core)
    input_grad = local(
        home_kernel, shaped(OWN, GROUPS * SPREAD, WIDTH, dtype=F32), [SMEM, VMEM, VMEM], core, got, out_grad
    )
    chunk = shaped(CHUNK, WIDTH)
    total = local(sum_kernel, chunk, [VMEM], got)
    total = local(round_kernel, chunk, [VMEM] * 4, total, *across(total, (1, 8, 9)))
    sent, gains = local(
        last_round_kernel,
        (shaped(CHIPS, ROWS, WIDTH), shaped(GAIN_ROWS, WIDTH)),
        [VMEM] * 4,
        total,
        *across(total, (2, 4, 6)),
    )
    mine = swap(sent, "member", same_core).reshape(CHIPS * ROWS, WIDTH)
    theirs = lax.ppermute(mine, "member", other_core)
    scale = 1.0 / math.sqrt(MEMBERS * GROUPS * SPREAD * spaces)
    square = shaped(WIDTH, WIDTH, dtype=F32)
    row = shaped(1, WIDTH, dtype=F32)
    grads = local(
        functools.partial(final_kernel, scale),
        (square, square, square, square, shaped(WIDTH, HIDDEN, dtype=F32), shaped(HIDDEN, WIDTH, dtype=F32), row, row),
        [SMEM, VMEM, VMEM, VMEM],
        core,
        mine,
        theirs,
        gains,
    )
    return (input_grad, *grads[:6], grads[6].reshape(WIDTH), grads[7].reshape(WIDTH))


def solution(mesh):
    in_specs = (
        P("member", "space", None),
        P("member", "space", None),
        P(),
        P(),
        P(),
        P(),
        P(),
        P(),
        P(),
        P(),
    )
    out_specs = (P("member", "space", None), P(), P(), P(), P(), P(), P(), P(), P())
    return jax.shard_map(
        on_device, mesh=mesh, in_specs=in_specs, out_specs=out_specs, check_vma=False
    )
```

```python
import functools
import math

import jax
import jax.numpy as jnp
from jax import lax
from jax.experimental import pallas as pl
from jax.experimental.pallas import tpu as pltpu
from jax.sharding import PartitionSpec as P

HEAD_DIM = 32
WIDTH = 256
HIDDEN = 1024
HEADS = WIDTH // HEAD_DIM
GROUPS = 16
CHIPS = 8
OWN = 4
SPREAD = 16
MEMBERS = GROUPS * OWN
TOKENS = MEMBERS * SPREAD
PIECE = OWN * SPREAD
HALF = WIDTH // 2
HALF_HEADS = HEADS // 2
LANES = HALF_HEADS * MEMBERS
ROWS = 192
GAIN_ROWS = 8
CHUNK = ROWS + GAIN_ROWS
SLAB = 24
SMALL = SLAB + GAIN_ROWS

EPS = 1e-06
GELU_C = 0.7978845608028654
GELU_A = 0.044715
SCALE = 1.0 / math.sqrt(HEAD_DIM)

F32 = jnp.float32
B16 = jnp.bfloat16
VMEM = pl.BlockSpec(memory_space=pltpu.VMEM)
HBM = pl.BlockSpec(memory_space=pltpu.HBM)
SMEM = pl.BlockSpec(memory_space=pltpu.SMEM)


def dot(left, right, contract):
    return lax.dot_general(left, right, ((contract[:1], contract[1:]), ((), ())), preferred_element_type=F32)


def norm_rows(values):
    inverse = lax.rsqrt(jnp.mean(values * values, axis=-1, keepdims=True) + EPS)
    return values * inverse, inverse


def norm_back(unit_rows, inverse, gains, upstream):
    scaled = upstream * gains
    return inverse * (scaled - unit_rows * jnp.mean(scaled * unit_rows, axis=-1, keepdims=True))


def gelu_pair(preact):
    square = preact * preact
    half = 0.5 + 0.5 * jnp.tanh(preact * (GELU_C + (GELU_C * GELU_A) * square))
    bend = preact * (2.0 * GELU_C + (6.0 * GELU_C * GELU_A) * square)
    return preact * half, half + (half - half * half) * bend


def own_heads(stacked):
    lane_head = lax.broadcasted_iota(jnp.int32, (MEMBERS, HALF), 1) // HEAD_DIM
    result = stacked[:MEMBERS]
    for head in range(1, HALF_HEADS):
        result = jnp.where(lane_head == head, stacked[head * MEMBERS : (head + 1) * MEMBERS], result)
    return result


def layer_kernel(
    core_ref,
    both_ref,
    gain1_ref,
    wqkv_ref,
    wout_ref,
    gain2_ref,
    wup_ref,
    wdown_ref,
    keep_ref,
    give_ref,
    xs,
    gs,
    ds,
    mask,
    qkv,
    expanded,
    probs,
    dprobs,
    rounded,
    mixs,
    gmix,
    n1s,
    n2s,
    gas,
    ogs,
    gqkv,
    gpre,
    acts,
    unit1s,
    unit2s,
    backs,
    products,
    wide_products,
    parts,
):
    core = core_ref[0]
    halves = [slice(side * HALF, (side + 1) * HALF) for side in range(2)]
    blocks = [slice(patch * MEMBERS, (patch + 1) * MEMBERS) for patch in range(SPREAD)]
    for group in range(GROUPS):
        rows = slice(group * PIECE, (group + 1) * PIECE)
        for side, lanes in enumerate(halves):
            xs[side, rows] = both_ref[group, 0, :, :, lanes].astype(F32).reshape(PIECE, HALF)
            gs[side, rows] = both_ref[group, 1, :, :, lanes].astype(F32).reshape(PIECE, HALF)
    mask[...] = (
        lax.broadcasted_iota(jnp.int32, (LANES, HALF), 0) // MEMBERS
        == lax.broadcasted_iota(jnp.int32, (LANES, HALF), 1) // HEAD_DIM
    ).astype(F32).astype(B16)
    gain1 = gain1_ref[...]
    gain2 = gain2_ref[...]

    def patch_rows(ref, patch):
        return jnp.concatenate(
            [ref[side, pl.ds(patch, MEMBERS, stride=SPREAD), :] for side in range(2)], axis=1
        )

    def spread_heads(rows):
        return jnp.concatenate([rows] * HALF_HEADS, axis=0) * mask[...]

    inverse1 = []
    for patch, rows in enumerate(blocks):
        unit, inverse = norm_rows(patch_rows(xs, patch))
        unit1s[rows] = unit
        inverse1.append(inverse)
        n1s[rows] = (unit * gain1).astype(B16)
        ogs[rows] = patch_rows(gs, patch).astype(B16)
    for i in range(3):
        lanes = slice(i * WIDTH, (i + 1) * WIDTH)
        qkv[:, lanes] = jnp.dot(n1s[...], wqkv_ref[:, lanes], preferred_element_type=F32).astype(B16)

    units = [(patch, side) for patch in range(SPREAD) for side in range(2)]

    def part(ref, index, patch, side):
        return ref[blocks[patch], index * WIDTH + side * HALF : index * WIDTH + (side + 1) * HALF]

    def staged(stages):
        lag = 4
        for step in range(0, len(units) + lag * (len(stages) - 1), lag):
            for late, stage in enumerate(stages):
                for unit in units[max(step - lag * late, 0) : max(step - lag * late + lag, 0)]:
                    stage(*unit)

    def score(patch, side):
        spread_query = spread_heads(part(qkv, 0, patch, side))
        expanded[patch, side] = spread_query
        probs[patch, side] = dot(part(qkv, 1, patch, side), spread_query, (1, 1)) * SCALE

    def soften(patch, side):
        scores = probs[patch, side]
        scores = jnp.exp(scores - jnp.max(scores, axis=0, keepdims=True))
        weights = scores * (1.0 / jnp.sum(scores, axis=0, keepdims=True))
        probs[patch, side] = weights
        rounded[patch, side] = weights.astype(B16)

    def mix(patch, side):
        mixed = own_heads(dot(rounded[patch, side], part(qkv, 2, patch, side), (0, 0)))
        mixs[blocks[patch], halves[side]] = mixed.astype(B16)

    staged((score, soften, mix))
    products[...] = jnp.dot(mixs[...], wout_ref[...], preferred_element_type=F32)
    inverse2 = []
    for patch, rows in enumerate(blocks):
        unit, inverse = norm_rows(patch_rows(xs, patch) + products[rows])
        unit2s[rows] = unit
        inverse2.append(inverse)
        n2s[rows] = (unit * gain2).astype(B16)

    for i in range(HIDDEN // WIDTH):
        lanes = slice(i * WIDTH, (i + 1) * WIDTH)
        wide_products[i % 2, 0] = jnp.dot(n2s[...], wup_ref[:, lanes], preferred_element_type=F32)
        wide_products[i % 2, 1] = dot(ogs[...], wdown_ref[lanes], (1, 1))
        for rows in blocks:
            activated, slopes = gelu_pair(wide_products[i % 2, 0, rows])
            acts[rows, lanes] = activated.astype(B16)
            gpre[rows, lanes] = (wide_products[i % 2, 1, rows] * slopes).astype(B16)
    products[...] = dot(gpre[...], wup_ref[...], (1, 1))
    gain2_sum = jnp.zeros((MEMBERS, WIDTH), F32)
    for patch, rows in enumerate(blocks):
        unit, grad = unit2s[rows], products[rows]
        gain2_sum = gain2_sum + grad * unit
        back = norm_back(unit, inverse2[patch], gain2, grad)
        backs[rows] = back
        gas[rows] = (ogs[rows].astype(F32) + back).astype(B16)
    gmix[...] = dot(gas[...], wout_ref[...], (1, 1)).astype(B16)

    def keep_grad(index, patch, side, grad):
        gqkv[blocks[patch], index * WIDTH + side * HALF : index * WIDTH + (side + 1) * HALF] = grad.astype(B16)

    def meet(patch, side):
        spread_grad = spread_heads(gmix[blocks[patch], halves[side]])
        dprobs[patch, side] = dot(part(qkv, 2, patch, side), spread_grad, (1, 1))
        keep_grad(2, patch, side, jnp.dot(rounded[patch, side], spread_grad, preferred_element_type=F32))

    def bend(patch, side):
        weights = probs[patch, side]
        product = weights * dprobs[patch, side]
        dscore = (product - weights * jnp.sum(product, axis=0, keepdims=True)) * SCALE
        rounded[patch, side] = dscore.astype(B16)

    def finish(patch, side):
        dscore = rounded[patch, side]
        keep_grad(1, patch, side, jnp.dot(dscore, expanded[patch, side], preferred_element_type=F32))
        keep_grad(0, patch, side, own_heads(dot(dscore, part(qkv, 1, patch, side), (0, 0))))

    def keep_part(first, total):
        rows = total.shape[0] // 2
        for half in range(2):
            parts[half, first : first + rows] = total[half * rows : (half + 1) * rows].astype(B16)

    for i in range(HIDDEN // WIDTH):
        lanes = slice(i * WIDTH, (i + 1) * WIDTH)
        keep_part(4 * HALF + i * HALF, dot(n2s[...], gpre[:, lanes], (0, 0)))
        first = 8 * HALF + i % 2 * WIDTH
        parts[i // 2, first : first + WIDTH] = dot(ogs[...], acts[:, lanes], (0, 0)).T.astype(B16)
    staged((meet, bend, finish))
    products[...] = dot(gqkv[...], wqkv_ref[...], (1, 1))
    gain1_sum = jnp.zeros((MEMBERS, WIDTH), F32)
    for patch, rows in enumerate(blocks):
        unit, grad = unit1s[rows], products[rows]
        gain1_sum = gain1_sum + grad * unit
        delta = backs[rows] + norm_back(unit, inverse1[patch], gain1, grad)
        for side, lanes in enumerate(halves):
            ds[side, pl.ds(patch, MEMBERS, stride=SPREAD), :] = delta[:, lanes]

    part_qkv = dot(n1s[...], gqkv[...], (0, 0))
    for i in range(3):
        keep_part(i * HALF, part_qkv[:, i * WIDTH : (i + 1) * WIDTH])
    keep_part(3 * HALF, dot(mixs[...], gas[...], (0, 0)))
    gain_rows = jnp.concatenate(
        [jnp.sum(total, axis=0, keepdims=True) for total in (gain1_sum, gain2_sum)]
        + [jnp.zeros((GAIN_ROWS - 2, WIDTH), F32)],
        axis=0,
    ).astype(B16)
    for target, side in ((keep_ref, core), (give_ref, 1 - core)):
        for chip in range(CHIPS):
            target[chip, :ROWS] = parts[side, chip * ROWS : (chip + 1) * ROWS]
            target[chip, ROWS:CHUNK] = gain_rows
            start = pl.multiple_of((2 * chip + side) * PIECE, PIECE)
            for half, lanes in enumerate(halves):
                target[chip, CHUNK:, lanes] = ds[half, pl.ds(start, PIECE)].astype(B16)


def run_layer(core, both, gain1, wqkv, wout, gain2, wup, wdown):
    rows = (TOKENS, WIDTH)
    scratch = [
        pltpu.VMEM((2, TOKENS, HALF), F32),
        pltpu.VMEM((2, TOKENS, HALF), F32),
        pltpu.VMEM((2, TOKENS, HALF), F32),
        pltpu.VMEM((LANES, HALF), B16),
        pltpu.VMEM((TOKENS, 3 * WIDTH), B16),
        pltpu.VMEM((SPREAD, 2, LANES, HALF), B16),
        pltpu.VMEM((SPREAD, 2, MEMBERS, LANES), F32),
        pltpu.VMEM((SPREAD, 2, MEMBERS, LANES), F32),
        pltpu.VMEM((SPREAD, 2, MEMBERS, LANES), B16),
        pltpu.VMEM(rows, B16),
        pltpu.VMEM(rows, B16),
        pltpu.VMEM(rows, B16),
        pltpu.VMEM(rows, B16),
        pltpu.VMEM(rows, B16),
        pltpu.VMEM(rows, B16),
        pltpu.VMEM((TOKENS, 3 * WIDTH), B16),
        pltpu.VMEM((TOKENS, HIDDEN), B16),
        pltpu.VMEM((TOKENS, HIDDEN), B16),
        pltpu.VMEM(rows, F32),
        pltpu.VMEM(rows, F32),
        pltpu.VMEM(rows, F32),
        pltpu.VMEM(rows, F32),
        pltpu.VMEM((2, 2, *rows), F32),
        pltpu.VMEM((2, CHIPS * ROWS, WIDTH), B16),
    ]
    shape = shaped(CHIPS, CHUNK + PIECE, WIDTH)
    return pl.pallas_call(
        layer_kernel,
        out_shape=(shape, shape),
        in_specs=[SMEM] + [VMEM] * 7,
        out_specs=(VMEM, VMEM),
        scratch_shapes=scratch,
        compiler_params=pltpu.CompilerParams(vmem_limit_bytes=48 * 1024 * 1024),
        cost_estimate=pl.CostEstimate(flops=5_000_000_000, bytes_accessed=6_000_000, transcendentals=2_000_000),
    )(core, both, gain1, wqkv, wout, gain2, wup, wdown)


def pack_kernel(input_ref, grad_ref, out_ref, held, in_sems, out_sems):
    pairs = []
    for own in range(OWN):
        for side, ref in enumerate((input_ref, grad_ref)):
            pairs.append(
                (
                    pltpu.make_async_copy(ref.at[own], held.at[side, own], in_sems.at[side, own]),
                    pltpu.make_async_copy(
                        held.at[side, own].reshape(GROUPS, SPREAD, WIDTH),
                        out_ref.at[:, side, own],
                        out_sems.at[side, own],
                    ),
                )
            )
    for arrive, _ in pairs:
        arrive.start()
    for arrive, leave in pairs:
        arrive.wait()
        leave.start()
    for _, leave in pairs:
        leave.wait()


def pack(layer_input, out_grad):
    return pl.pallas_call(
        pack_kernel,
        out_shape=shaped(GROUPS, 2, OWN, SPREAD, WIDTH),
        in_specs=[HBM, HBM],
        out_specs=HBM,
        scratch_shapes=[
            pltpu.VMEM((2, OWN, GROUPS * SPREAD, WIDTH), B16),
            pltpu.SemaphoreType.DMA((2, OWN)),
            pltpu.SemaphoreType.DMA((2, OWN)),
        ],
    )(layer_input, out_grad)


def pair_kernel(keep_ref, got_ref, out_ref):
    for chip in range(CHIPS):
        total = keep_ref[chip, :CHUNK].astype(F32) + got_ref[chip, :CHUNK].astype(F32)
        out_ref[chip, :CHUNK] = total.astype(B16)
        out_ref[chip, CHUNK : CHUNK + PIECE] = keep_ref[chip, CHUNK:]
        out_ref[chip, CHUNK + PIECE :] = got_ref[chip, CHUNK:]


def sum_kernel(got_ref, out_ref):
    total = got_ref[0, :CHUNK].astype(F32)
    for chip in range(1, CHIPS):
        total = total + got_ref[chip, :CHUNK].astype(F32)
    out_ref[...] = total.astype(B16)


def four(refs):
    own, first, second, third = (ref[...].astype(F32) for ref in refs)
    return ((own + first) + (second + third)).astype(B16)


def round_kernel(own_ref, first_ref, second_ref, third_ref, out_ref):
    out_ref[...] = four((own_ref, first_ref, second_ref, third_ref))


def last_round_kernel(own_ref, first_ref, second_ref, third_ref, done_ref, out_ref, gains_ref):
    del done_ref
    total = four((own_ref, first_ref, second_ref, third_ref))
    for chip in range(CHIPS):
        out_ref[chip] = total[:ROWS]
    gains_ref[...] = total[ROWS:]


def home_kernel(core_ref, got_ref, grad_ref, out_ref, done_ref):
    done_ref[...] = jnp.zeros_like(done_ref)
    core = core_ref[0]
    for chip in range(CHIPS):
        for part in range(2):
            index = 2 * chip + (core if part == 0 else 1 - core)
            there = pl.ds(pl.multiple_of(index * SPREAD, SPREAD), SPREAD)
            first = CHUNK + part * PIECE
            for own in range(OWN):
                moved = got_ref[chip, first + own * SPREAD : first + (own + 1) * SPREAD]
                out_ref[own, there] = grad_ref[own, there].astype(F32) + moved.astype(F32)


def write_half(scale, side, part_ref, out_refs, held, held_up, sems):
    copies = []

    def send(source, out_ref, rows, index):
        there = pl.ds(pl.multiple_of(side * rows, rows), rows)
        copies.append(pltpu.make_async_copy(source, out_ref.at[there], sems.at[index]))
        copies[-1].start()

    for index in range(4):
        rows = slice(index * HALF, (index + 1) * HALF)
        held[rows] = part_ref[rows].astype(F32) * scale
        send(held.at[rows], out_refs[index], HALF, index)
    for index in range(HIDDEN // WIDTH):
        first = (4 + index) * HALF
        held_up[:, index * WIDTH : (index + 1) * WIDTH] = part_ref[first : first + HALF].astype(F32) * scale
    send(held_up, out_refs[4], HALF, 4)
    rows = slice(8 * HALF, 12 * HALF)
    held[rows] = part_ref[rows].astype(F32) * scale
    send(held.at[rows], out_refs[5], 4 * HALF, 5)
    for copy in copies:
        copy.wait()


def mine_kernel(scale, core_ref, part_ref, gains_ref, *refs):
    refs[6][...] = gains_ref[0:1].astype(F32) * scale
    refs[7][...] = gains_ref[1:2].astype(F32) * scale
    write_half(scale, core_ref[0], part_ref, refs[:6], *refs[8:])


def theirs_kernel(scale, core_ref, part_ref, *refs):
    write_half(scale, 1 - core_ref[0], part_ref, refs[6:12], *refs[12:])


FINAL_SCRATCH = (
    pltpu.VMEM((CHIPS * ROWS, WIDTH), F32),
    pltpu.VMEM((HALF, HIDDEN), F32),
    pltpu.SemaphoreType.DMA((6,)),
)


def local(kernel, out_shape, specs, *operands):
    return pl.pallas_call(
        kernel,
        out_shape=out_shape,
        in_specs=specs,
        out_specs=jax.tree.map(lambda _: VMEM, out_shape),
        compiler_params=pltpu.CompilerParams(vmem_limit_bytes=32 * 1024 * 1024),
    )(*operands)


def shaped(*shape, dtype=B16):
    return jax.ShapeDtypeStruct(shape, dtype)


def swap(array, axis, groups=None):
    return lax.all_to_all(
        array, axis, split_axis=0, concat_axis=0, tiled=True, axis_index_groups=groups
    )


def on_device(
    layer_input, out_grad, norm1_gain, w_query, w_key, w_value, w_out, norm2_gain, w_up, w_down
):
    members = lax.axis_size("member")
    spaces = lax.axis_size("space")
    core = (lax.axis_index("member") % 2).astype(jnp.int32).reshape(1)
    other_core = [(k, k ^ 1) for k in range(members)]
    same_core = [[c + 2 * k for k in range(CHIPS)] for c in range(2)]

    def across(array, steps):
        return [lax.ppermute(array, "space", [(k, k ^ step) for k in range(spaces)]) for step in steps]

    both = swap(pack(layer_input, out_grad), "member")
    wqkv = jnp.concatenate([w_query, w_key, w_value], axis=1)
    keep, give = run_layer(
        core, both, norm1_gain.reshape(1, WIDTH), wqkv, w_out, norm2_gain.reshape(1, WIDTH), w_up, w_down
    )
    got = lax.ppermute(give, "member", other_core)
    sent = local(pair_kernel, shaped(CHIPS, CHUNK + 2 * PIECE, WIDTH), [VMEM] * 2, keep, got)
    got = swap(sent, "member", same_core)
    input_grad, done = local(
        home_kernel,
        (shaped(OWN, GROUPS * SPREAD, WIDTH, dtype=F32), shaped(8, HALF, dtype=F32)),
        [SMEM, VMEM, VMEM],
        core,
        got,
        out_grad,
    )
    chunk = shaped(CHUNK, WIDTH)
    total = local(sum_kernel, chunk, [VMEM], got)
    total = local(round_kernel, chunk, [VMEM] * 4, total, *across(total, (1, 8, 9)))
    sent, gains = local(
        last_round_kernel,
        (shaped(CHIPS, ROWS, WIDTH), shaped(GAIN_ROWS, WIDTH)),
        [VMEM] * 5,
        total,
        *across(total, (2, 4, 6)),
        done,
    )
    mine = swap(sent, "member", same_core).reshape(CHIPS * ROWS, WIDTH)
    theirs = lax.ppermute(mine, "member", other_core)
    scale = 1.0 / math.sqrt(MEMBERS * GROUPS * SPREAD * spaces)
    square = shaped(WIDTH, WIDTH, dtype=F32)
    row = shaped(1, WIDTH, dtype=F32)
    grads_shape = (square, square, square, square, shaped(WIDTH, HIDDEN, dtype=F32), shaped(HIDDEN, WIDTH, dtype=F32))
    params = pltpu.CompilerParams(vmem_limit_bytes=32 * 1024 * 1024)
    *grads, gain1, gain2 = pl.pallas_call(
        functools.partial(mine_kernel, scale),
        out_shape=(*grads_shape, row, row),
        in_specs=[SMEM, VMEM, VMEM],
        out_specs=(*[HBM] * 6, VMEM, VMEM),
        scratch_shapes=FINAL_SCRATCH,
        compiler_params=params,
    )(core, mine, gains)
    grads = pl.pallas_call(
        functools.partial(theirs_kernel, scale),
        out_shape=grads_shape,
        in_specs=[SMEM, VMEM, *[HBM] * 6],
        out_specs=(HBM,) * 6,
        input_output_aliases={2 + index: index for index in range(6)},
        scratch_shapes=FINAL_SCRATCH,
        compiler_params=params,
    )(core, theirs, *grads)
    return (input_grad, *grads, gain1.reshape(WIDTH), gain2.reshape(WIDTH))


def solution(mesh):
    in_specs = (
        P("member", "space", None),
        P("member", "space", None),
        P(),
        P(),
        P(),
        P(),
        P(),
        P(),
        P(),
        P(),
    )
    out_specs = (P("member", "space", None), P(), P(), P(), P(), P(), P(), P(), P())
    return jax.shard_map(
        on_device, mesh=mesh, in_specs=in_specs, out_specs=out_specs, check_vma=False
    )
```

```python
import functools
import math

import jax
import jax.numpy as jnp
from jax import lax
from jax.experimental import pallas as pl
from jax.experimental.pallas import tpu as pltpu
from jax.sharding import PartitionSpec as P

HEAD_DIM = 32
WIDTH = 256
HIDDEN = 1024
HEADS = WIDTH // HEAD_DIM
GROUPS = 16
CHIPS = 8
OWN = 4
SPREAD = 16
MEMBERS = GROUPS * OWN
TOKENS = MEMBERS * SPREAD
PIECE = OWN * SPREAD
HALF = WIDTH // 2
HALF_HEADS = HEADS // 2
LANES = HALF_HEADS * MEMBERS
GROUP = 8
ROWS = 192
GAIN_ROWS = 8
CHUNK = ROWS + GAIN_ROWS
SLAB = 24
SMALL = SLAB + GAIN_ROWS

EPS = 1e-06
GELU_C = 0.7978845608028654
GELU_A = 0.044715
SCALE = 1.0 / math.sqrt(HEAD_DIM)

F32 = jnp.float32
B16 = jnp.bfloat16
VMEM = pl.BlockSpec(memory_space=pltpu.VMEM)
HBM = pl.BlockSpec(memory_space=pltpu.HBM)
SMEM = pl.BlockSpec(memory_space=pltpu.SMEM)


def dot(left, right, contract):
    return lax.dot_general(left, right, ((contract[:1], contract[1:]), ((), ())), preferred_element_type=F32)


def norm_rows(values):
    inverse = lax.rsqrt(jnp.mean(values * values, axis=-1, keepdims=True) + EPS)
    return values * inverse, inverse


def norm_back(unit_rows, inverse, gains, upstream):
    scaled = upstream * gains
    return inverse * (scaled - unit_rows * jnp.mean(scaled * unit_rows, axis=-1, keepdims=True))


def gelu_pair(preact):
    square = preact * preact
    half = 0.5 + 0.5 * jnp.tanh(preact * (GELU_C + (GELU_C * GELU_A) * square))
    bend = preact * (2.0 * GELU_C + (6.0 * GELU_C * GELU_A) * square)
    return preact * half, half + (half - half * half) * bend


def own_heads(stacked):
    lane_head = lax.broadcasted_iota(jnp.int32, (MEMBERS, HALF), 1) // HEAD_DIM
    result = stacked[:MEMBERS]
    for head in range(1, HALF_HEADS):
        result = jnp.where(lane_head == head, stacked[head * MEMBERS : (head + 1) * MEMBERS], result)
    return result


def layer_kernel(
    core_ref,
    both_ref,
    gain1_ref,
    wqkv_ref,
    wout_ref,
    gain2_ref,
    wup_ref,
    wdown_ref,
    keep_ref,
    give_ref,
    xs,
    gs,
    ds,
    mask,
    qkv,
    expanded,
    probs,
    dprobs,
    rounded,
    mixs,
    gmix,
    n1s,
    n2s,
    gas,
    ogs,
    gqkv,
    gpre,
    acts,
    unit1s,
    unit2s,
    backs,
    products,
    wide_products,
    parts,
):
    core = core_ref[0]
    halves = [slice(side * HALF, (side + 1) * HALF) for side in range(2)]
    blocks = [slice(patch * MEMBERS, (patch + 1) * MEMBERS) for patch in range(SPREAD)]
    for group in range(GROUPS):
        rows = slice(group * PIECE, (group + 1) * PIECE)
        for side, lanes in enumerate(halves):
            xs[side, rows] = both_ref[group, 0, :, :, lanes].astype(F32).reshape(PIECE, HALF)
            gs[side, rows] = both_ref[group, 1, :, :, lanes].astype(F32).reshape(PIECE, HALF)
    mask[...] = (
        lax.broadcasted_iota(jnp.int32, (LANES, HALF), 0) // MEMBERS
        == lax.broadcasted_iota(jnp.int32, (LANES, HALF), 1) // HEAD_DIM
    ).astype(F32).astype(B16)
    gain1 = gain1_ref[...]
    gain2 = gain2_ref[...]

    def patch_rows(ref, patch):
        return jnp.concatenate(
            [ref[side, pl.ds(patch, MEMBERS, stride=SPREAD), :] for side in range(2)], axis=1
        )

    def spread_heads(rows):
        return jnp.concatenate([rows] * HALF_HEADS, axis=0) * mask[...]

    inverse1, inverse2 = {}, {}
    gain_sums = [jnp.zeros((MEMBERS, WIDTH), F32), jnp.zeros((MEMBERS, WIDTH), F32)]
    rows_of = [slice(first, first + GROUP * MEMBERS) for first in range(0, TOKENS, GROUP * MEMBERS)]
    groups = [range(first, first + GROUP) for first in range(0, SPREAD, GROUP)]

    def part(ref, index, patch, side):
        return ref[blocks[patch], index * WIDTH + side * HALF : index * WIDTH + (side + 1) * HALF]

    def keep_grad(index, patch, side, grad):
        gqkv[blocks[patch], index * WIDTH + side * HALF : index * WIDTH + (side + 1) * HALF] = grad.astype(B16)

    def keep_part(first, total):
        rows = total.shape[0] // 2
        for half in range(2):
            parts[half, first : first + rows] = total[half * rows : (half + 1) * rows].astype(B16)

    def first_norm(group):
        for patch in groups[group]:
            rows = blocks[patch]
            unit, inverse1[patch] = norm_rows(patch_rows(xs, patch))
            unit1s[rows] = unit
            n1s[rows] = (unit * gain1).astype(B16)
            ogs[rows] = patch_rows(gs, patch).astype(B16)

    def project(group):
        rows = rows_of[group]
        for i in range(3):
            lanes = slice(i * WIDTH, (i + 1) * WIDTH)
            qkv[rows, lanes] = jnp.dot(n1s[rows], wqkv_ref[:, lanes], preferred_element_type=F32).astype(B16)

    def score(group):
        for patch in groups[group]:
            for side in range(2):
                spread_query = spread_heads(part(qkv, 0, patch, side))
                expanded[patch, side] = spread_query
                probs[patch, side] = dot(part(qkv, 1, patch, side), spread_query, (1, 1)) * SCALE

    def soften(group):
        for patch in groups[group]:
            for side in range(2):
                scores = probs[patch, side]
                scores = jnp.exp(scores - jnp.max(scores, axis=0, keepdims=True))
                weights = scores * (1.0 / jnp.sum(scores, axis=0, keepdims=True))
                probs[patch, side] = weights
                rounded[patch, side] = weights.astype(B16)

    def mix(group):
        for patch in groups[group]:
            for side in range(2):
                mixed = own_heads(dot(rounded[patch, side], part(qkv, 2, patch, side), (0, 0)))
                mixs[blocks[patch], halves[side]] = mixed.astype(B16)

    def join(group):
        rows = rows_of[group]
        products[rows] = jnp.dot(mixs[rows], wout_ref[...], preferred_element_type=F32)

    def second_norm(group):
        for patch in groups[group]:
            rows = blocks[patch]
            unit, inverse2[patch] = norm_rows(patch_rows(xs, patch) + products[rows])
            unit2s[rows] = unit
            n2s[rows] = (unit * gain2).astype(B16)

    def rise(group):
        rows = rows_of[group]
        for i in range(HIDDEN // WIDTH):
            lanes = slice(i * WIDTH, (i + 1) * WIDTH)
            wide_products[group % 2, 0, :, lanes] = jnp.dot(n2s[rows], wup_ref[:, lanes], preferred_element_type=F32)
            wide_products[group % 2, 1, :, lanes] = dot(ogs[rows], wdown_ref[lanes], (1, 1))

    def curve(group):
        for i in range(HIDDEN // WIDTH):
            lanes = slice(i * WIDTH, (i + 1) * WIDTH)
            for index, patch in enumerate(groups[group]):
                here = slice(index * MEMBERS, (index + 1) * MEMBERS)
                activated, slopes = gelu_pair(wide_products[group % 2, 0, here, lanes])
                acts[blocks[patch], lanes] = activated.astype(B16)
                gpre[blocks[patch], lanes] = (wide_products[group % 2, 1, here, lanes] * slopes).astype(B16)

    def fall(group):
        rows = rows_of[group]
        products[rows] = dot(gpre[rows], wup_ref[...], (1, 1))

    def second_back(group):
        for patch in groups[group]:
            rows = blocks[patch]
            unit, grad = unit2s[rows], products[rows]
            gain_sums[1] = gain_sums[1] + grad * unit
            back = norm_back(unit, inverse2[patch], gain2, grad)
            backs[rows] = back
            gas[rows] = (ogs[rows].astype(F32) + back).astype(B16)

    def part_back(group):
        rows = rows_of[group]
        gmix[rows] = dot(gas[rows], wout_ref[...], (1, 1)).astype(B16)

    def meet(group):
        for patch in groups[group]:
            for side in range(2):
                spread_grad = spread_heads(gmix[blocks[patch], halves[side]])
                dprobs[patch, side] = dot(part(qkv, 2, patch, side), spread_grad, (1, 1))
                keep_grad(2, patch, side, jnp.dot(rounded[patch, side], spread_grad, preferred_element_type=F32))

    def bend(group):
        for patch in groups[group]:
            for side in range(2):
                weights = probs[patch, side]
                product = weights * dprobs[patch, side]
                dscore = (product - weights * jnp.sum(product, axis=0, keepdims=True)) * SCALE
                rounded[patch, side] = dscore.astype(B16)

    def finish(group):
        for patch in groups[group]:
            for side in range(2):
                dscore = rounded[patch, side]
                keep_grad(1, patch, side, jnp.dot(dscore, expanded[patch, side], preferred_element_type=F32))
                keep_grad(0, patch, side, own_heads(dot(dscore, part(qkv, 1, patch, side), (0, 0))))

    def first_fall(group):
        rows = rows_of[group]
        products[rows] = dot(gqkv[rows], wqkv_ref[...], (1, 1))

    def first_back(group):
        for patch in groups[group]:
            rows = blocks[patch]
            unit, grad = unit1s[rows], products[rows]
            gain_sums[0] = gain_sums[0] + grad * unit
            delta = backs[rows] + norm_back(unit, inverse1[patch], gain1, grad)
            for side, lanes in enumerate(halves):
                ds[side, pl.ds(patch, MEMBERS, stride=SPREAD), :] = delta[:, lanes]

    def weigh(i):
        lanes = slice(i * WIDTH, (i + 1) * WIDTH)
        keep_part(4 * HALF + i * HALF, dot(n2s[...], gpre[:, lanes], (0, 0)))
        first = 8 * HALF + i % 2 * WIDTH
        parts[i // 2, first : first + WIDTH] = dot(ogs[...], acts[:, lanes], (0, 0)).T.astype(B16)

    stages = (
        first_norm, project, score, soften, mix, join, second_norm, rise, curve,
        fall, second_back, part_back, meet, bend, finish, first_fall, first_back,
    )
    weigh_from = len(groups) + stages.index(curve)
    for step in range(len(groups) + len(stages) - 1):
        for late, stage in enumerate(stages):
            if 0 <= step - late < len(groups):
                stage(step - late)
        if 0 <= step - weigh_from < HIDDEN // WIDTH:
            weigh(step - weigh_from)
    gain1_sum, gain2_sum = gain_sums

    part_qkv = dot(n1s[...], gqkv[...], (0, 0))
    for i in range(3):
        keep_part(i * HALF, part_qkv[:, i * WIDTH : (i + 1) * WIDTH])
    keep_part(3 * HALF, dot(mixs[...], gas[...], (0, 0)))
    gain_rows = jnp.concatenate(
        [jnp.sum(total, axis=0, keepdims=True) for total in (gain1_sum, gain2_sum)]
        + [jnp.zeros((GAIN_ROWS - 2, WIDTH), F32)],
        axis=0,
    ).astype(B16)
    for target, side in ((keep_ref, core), (give_ref, 1 - core)):
        for chip in range(CHIPS):
            target[chip, :ROWS] = parts[side, chip * ROWS : (chip + 1) * ROWS]
            target[chip, ROWS:CHUNK] = gain_rows
            start = pl.multiple_of((2 * chip + side) * PIECE, PIECE)
            for half, lanes in enumerate(halves):
                target[chip, CHUNK:, lanes] = ds[half, pl.ds(start, PIECE)].astype(B16)


def run_layer(core, both, gain1, wqkv, wout, gain2, wup, wdown):
    rows = (TOKENS, WIDTH)
    scratch = [
        pltpu.VMEM((2, TOKENS, HALF), F32),
        pltpu.VMEM((2, TOKENS, HALF), F32),
        pltpu.VMEM((2, TOKENS, HALF), F32),
        pltpu.VMEM((LANES, HALF), B16),
        pltpu.VMEM((TOKENS, 3 * WIDTH), B16),
        pltpu.VMEM((SPREAD, 2, LANES, HALF), B16),
        pltpu.VMEM((SPREAD, 2, MEMBERS, LANES), F32),
        pltpu.VMEM((SPREAD, 2, MEMBERS, LANES), F32),
        pltpu.VMEM((SPREAD, 2, MEMBERS, LANES), B16),
        pltpu.VMEM(rows, B16),
        pltpu.VMEM(rows, B16),
        pltpu.VMEM(rows, B16),
        pltpu.VMEM(rows, B16),
        pltpu.VMEM(rows, B16),
        pltpu.VMEM(rows, B16),
        pltpu.VMEM((TOKENS, 3 * WIDTH), B16),
        pltpu.VMEM((TOKENS, HIDDEN), B16),
        pltpu.VMEM((TOKENS, HIDDEN), B16),
        pltpu.VMEM(rows, F32),
        pltpu.VMEM(rows, F32),
        pltpu.VMEM(rows, F32),
        pltpu.VMEM(rows, F32),
        pltpu.VMEM((2, 2, GROUP * MEMBERS, HIDDEN), F32),
        pltpu.VMEM((2, CHIPS * ROWS, WIDTH), B16),
    ]
    shape = shaped(CHIPS, CHUNK + PIECE, WIDTH)
    return pl.pallas_call(
        layer_kernel,
        out_shape=(shape, shape),
        in_specs=[SMEM] + [VMEM] * 7,
        out_specs=(VMEM, VMEM),
        scratch_shapes=scratch,
        compiler_params=pltpu.CompilerParams(vmem_limit_bytes=48 * 1024 * 1024),
        cost_estimate=pl.CostEstimate(flops=5_000_000_000, bytes_accessed=6_000_000, transcendentals=2_000_000),
    )(core, both, gain1, wqkv, wout, gain2, wup, wdown)


def pack_kernel(input_ref, grad_ref, out_ref, held, in_sems, out_sems):
    pairs = []
    for own in range(OWN):
        for side, ref in enumerate((input_ref, grad_ref)):
            pairs.append(
                (
                    pltpu.make_async_copy(ref.at[own], held.at[side, own], in_sems.at[side, own]),
                    pltpu.make_async_copy(
                        held.at[side, own].reshape(GROUPS, SPREAD, WIDTH),
                        out_ref.at[:, side, own],
                        out_sems.at[side, own],
                    ),
                )
            )
    for arrive, _ in pairs:
        arrive.start()
    for arrive, leave in pairs:
        arrive.wait()
        leave.start()
    for _, leave in pairs:
        leave.wait()


def pack(layer_input, out_grad):
    return pl.pallas_call(
        pack_kernel,
        out_shape=shaped(GROUPS, 2, OWN, SPREAD, WIDTH),
        in_specs=[HBM, HBM],
        out_specs=HBM,
        scratch_shapes=[
            pltpu.VMEM((2, OWN, GROUPS * SPREAD, WIDTH), B16),
            pltpu.SemaphoreType.DMA((2, OWN)),
            pltpu.SemaphoreType.DMA((2, OWN)),
        ],
    )(layer_input, out_grad)


def pair_kernel(keep_ref, got_ref, out_ref):
    for chip in range(CHIPS):
        total = keep_ref[chip, :CHUNK].astype(F32) + got_ref[chip, :CHUNK].astype(F32)
        out_ref[chip, :CHUNK] = total.astype(B16)
        out_ref[chip, CHUNK : CHUNK + PIECE] = keep_ref[chip, CHUNK:]
        out_ref[chip, CHUNK + PIECE :] = got_ref[chip, CHUNK:]


def sum_kernel(got_ref, out_ref):
    total = got_ref[0, :CHUNK].astype(F32)
    for chip in range(1, CHIPS):
        total = total + got_ref[chip, :CHUNK].astype(F32)
    out_ref[...] = total.astype(B16)


def four(refs):
    own, first, second, third = (ref[...].astype(F32) for ref in refs)
    return ((own + first) + (second + third)).astype(B16)


def round_kernel(own_ref, first_ref, second_ref, third_ref, out_ref):
    out_ref[...] = four((own_ref, first_ref, second_ref, third_ref))


def last_round_kernel(own_ref, first_ref, second_ref, third_ref, done_ref, out_ref, gains_ref):
    del done_ref
    total = four((own_ref, first_ref, second_ref, third_ref))
    for chip in range(CHIPS):
        out_ref[chip] = total[:ROWS]
    gains_ref[...] = total[ROWS:]


def home_kernel(core_ref, got_ref, grad_ref, out_ref, done_ref):
    done_ref[...] = jnp.zeros_like(done_ref)
    core = core_ref[0]
    for chip in range(CHIPS):
        for part in range(2):
            index = 2 * chip + (core if part == 0 else 1 - core)
            there = pl.ds(pl.multiple_of(index * SPREAD, SPREAD), SPREAD)
            first = CHUNK + part * PIECE
            for own in range(OWN):
                moved = got_ref[chip, first + own * SPREAD : first + (own + 1) * SPREAD]
                out_ref[own, there] = grad_ref[own, there].astype(F32) + moved.astype(F32)


def write_half(scale, side, part_ref, out_refs, held, held_up, sems):
    copies = []

    def send(source, out_ref, rows, index):
        there = pl.ds(pl.multiple_of(side * rows, rows), rows)
        copies.append(pltpu.make_async_copy(source, out_ref.at[there], sems.at[index]))
        copies[-1].start()

    for index in range(4):
        rows = slice(index * HALF, (index + 1) * HALF)
        held[rows] = part_ref[rows].astype(F32) * scale
        send(held.at[rows], out_refs[index], HALF, index)
    for index in range(HIDDEN // WIDTH):
        first = (4 + index) * HALF
        held_up[:, index * WIDTH : (index + 1) * WIDTH] = part_ref[first : first + HALF].astype(F32) * scale
    send(held_up, out_refs[4], HALF, 4)
    rows = slice(8 * HALF, 12 * HALF)
    held[rows] = part_ref[rows].astype(F32) * scale
    send(held.at[rows], out_refs[5], 4 * HALF, 5)
    for copy in copies:
        copy.wait()


def mine_kernel(scale, core_ref, part_ref, gains_ref, *refs):
    refs[6][...] = gains_ref[0:1].astype(F32) * scale
    refs[7][...] = gains_ref[1:2].astype(F32) * scale
    write_half(scale, core_ref[0], part_ref, refs[:6], *refs[8:])


def theirs_kernel(scale, core_ref, part_ref, *refs):
    write_half(scale, 1 - core_ref[0], part_ref, refs[6:12], *refs[12:])


FINAL_SCRATCH = (
    pltpu.VMEM((CHIPS * ROWS, WIDTH), F32),
    pltpu.VMEM((HALF, HIDDEN), F32),
    pltpu.SemaphoreType.DMA((6,)),
)


def local(kernel, out_shape, specs, *operands):
    return pl.pallas_call(
        kernel,
        out_shape=out_shape,
        in_specs=specs,
        out_specs=jax.tree.map(lambda _: VMEM, out_shape),
        compiler_params=pltpu.CompilerParams(vmem_limit_bytes=32 * 1024 * 1024),
    )(*operands)


def shaped(*shape, dtype=B16):
    return jax.ShapeDtypeStruct(shape, dtype)


def swap(array, axis, groups=None):
    return lax.all_to_all(
        array, axis, split_axis=0, concat_axis=0, tiled=True, axis_index_groups=groups
    )


def on_device(
    layer_input, out_grad, norm1_gain, w_query, w_key, w_value, w_out, norm2_gain, w_up, w_down
):
    members = lax.axis_size("member")
    spaces = lax.axis_size("space")
    core = (lax.axis_index("member") % 2).astype(jnp.int32).reshape(1)
    other_core = [(k, k ^ 1) for k in range(members)]
    same_core = [[c + 2 * k for k in range(CHIPS)] for c in range(2)]

    def across(array, steps):
        return [lax.ppermute(array, "space", [(k, k ^ step) for k in range(spaces)]) for step in steps]

    both = swap(pack(layer_input, out_grad), "member")
    wqkv = jnp.concatenate([w_query, w_key, w_value], axis=1)
    keep, give = run_layer(
        core, both, norm1_gain.reshape(1, WIDTH), wqkv, w_out, norm2_gain.reshape(1, WIDTH), w_up, w_down
    )
    got = lax.ppermute(give, "member", other_core)
    sent = local(pair_kernel, shaped(CHIPS, CHUNK + 2 * PIECE, WIDTH), [VMEM] * 2, keep, got)
    got = swap(sent, "member", same_core)
    input_grad, done = local(
        home_kernel,
        (shaped(OWN, GROUPS * SPREAD, WIDTH, dtype=F32), shaped(8, HALF, dtype=F32)),
        [SMEM, VMEM, VMEM],
        core,
        got,
        out_grad,
    )
    chunk = shaped(CHUNK, WIDTH)
    total = local(sum_kernel, chunk, [VMEM], got)
    total = local(round_kernel, chunk, [VMEM] * 4, total, *across(total, (2, 4, 6) ))
    sent, gains = local(
        last_round_kernel,
        (shaped(CHIPS, ROWS, WIDTH), shaped(GAIN_ROWS, WIDTH)),
        [VMEM] * 5,
        total,
        *across(total, (1, 8, 9)),
        done,
    )
    mine = swap(sent, "member", same_core).reshape(CHIPS * ROWS, WIDTH)
    theirs = lax.ppermute(mine, "member", other_core)
    scale = 1.0 / math.sqrt(MEMBERS * GROUPS * SPREAD * spaces)
    square = shaped(WIDTH, WIDTH, dtype=F32)
    row = shaped(1, WIDTH, dtype=F32)
    grads_shape = (square, square, square, square, shaped(WIDTH, HIDDEN, dtype=F32), shaped(HIDDEN, WIDTH, dtype=F32))
    params = pltpu.CompilerParams(vmem_limit_bytes=32 * 1024 * 1024)
    *grads, gain1, gain2 = pl.pallas_call(
        functools.partial(mine_kernel, scale),
        out_shape=(*grads_shape, row, row),
        in_specs=[SMEM, VMEM, VMEM],
        out_specs=(*[HBM] * 6, VMEM, VMEM),
        scratch_shapes=FINAL_SCRATCH,
        compiler_params=params,
    )(core, mine, gains)
    grads = pl.pallas_call(
        functools.partial(theirs_kernel, scale),
        out_shape=grads_shape,
        in_specs=[SMEM, VMEM, *[HBM] * 6],
        out_specs=(HBM,) * 6,
        input_output_aliases={2 + index: index for index in range(6)},
        scratch_shapes=FINAL_SCRATCH,
        compiler_params=params,
    )(core, theirs, *grads)
    return (input_grad, *grads, gain1.reshape(WIDTH), gain2.reshape(WIDTH))


def solution(mesh):
    in_specs = (
        P("member", "space", None),
        P("member", "space", None),
        P(),
        P(),
        P(),
        P(),
        P(),
        P(),
        P(),
        P(),
    )
    out_specs = (P("member", "space", None), P(), P(), P(), P(), P(), P(), P(), P())
    return jax.shard_map(
        on_device, mesh=mesh, in_specs=in_specs, out_specs=out_specs, check_vma=False
    )
```

```python
import functools
import math

import jax
import jax.numpy as jnp
from jax import lax
from jax.experimental import pallas as pl
from jax.experimental.pallas import tpu as pltpu
from jax.sharding import PartitionSpec as P

HEAD_DIM = 32
WIDTH = 256
HIDDEN = 1024
HEADS = WIDTH // HEAD_DIM
GROUPS = 16
CHIPS = 8
OWN = 4
SPREAD = 16
MEMBERS = GROUPS * OWN
TOKENS = MEMBERS * SPREAD
PIECE = OWN * SPREAD
HALF = WIDTH // 2
HALF_HEADS = HEADS // 2
LANES = HALF_HEADS * MEMBERS
GROUP = 8
ROWS = 192
GAIN_ROWS = 16
CHUNK = ROWS + GAIN_ROWS
SLAB = 24
SMALL = SLAB + GAIN_ROWS

EPS = 1e-06
GELU_C = 0.7978845608028654
GELU_A = 0.044715
SCALE = 1.0 / math.sqrt(HEAD_DIM)

F32 = jnp.float32
B16 = jnp.bfloat16
VMEM = pl.BlockSpec(memory_space=pltpu.VMEM)
HBM = pl.BlockSpec(memory_space=pltpu.HBM)
SMEM = pl.BlockSpec(memory_space=pltpu.SMEM)


def dot(left, right, contract):
    return lax.dot_general(left, right, ((contract[:1], contract[1:]), ((), ())), preferred_element_type=F32)


def norm_rows(values):
    inverse = lax.rsqrt(jnp.mean(values * values, axis=-1, keepdims=True) + EPS)
    return values * inverse, inverse


def norm_back(unit_rows, inverse, gains, upstream):
    scaled = upstream * gains
    return inverse * (scaled - unit_rows * jnp.mean(scaled * unit_rows, axis=-1, keepdims=True))


def gelu_pair(preact):
    square = preact * preact
    half = 0.5 + 0.5 * jnp.tanh(preact * (GELU_C + (GELU_C * GELU_A) * square))
    bend = preact * (2.0 * GELU_C + (6.0 * GELU_C * GELU_A) * square)
    return preact * half, half + (half - half * half) * bend


def own_heads(stacked):
    lane_head = lax.broadcasted_iota(jnp.int32, (MEMBERS, HALF), 1) // HEAD_DIM
    result = stacked[:MEMBERS]
    for head in range(1, HALF_HEADS):
        result = jnp.where(lane_head == head, stacked[head * MEMBERS : (head + 1) * MEMBERS], result)
    return result


def layer_kernel(
    core_ref,
    both_ref,
    gain1_ref,
    wqkv_ref,
    wout_ref,
    gain2_ref,
    wup_ref,
    wdown_ref,
    keep_ref,
    give_ref,
    xs,
    gs,
    ds,
    mask,
    qkv,
    expanded,
    probs,
    dprobs,
    rounded,
    mixs,
    gmix,
    n1s,
    n2s,
    gas,
    ogs,
    gqkv,
    gpre,
    acts,
    unit1s,
    unit2s,
    backs,
    products,
    wide_products,
    parts,
):
    core = core_ref[0]
    halves = [slice(side * HALF, (side + 1) * HALF) for side in range(2)]
    blocks = [slice(patch * MEMBERS, (patch + 1) * MEMBERS) for patch in range(SPREAD)]
    for group in range(GROUPS):
        rows = slice(group * PIECE, (group + 1) * PIECE)
        for side, lanes in enumerate(halves):
            xs[side, rows] = both_ref[group, 0, :, :, lanes].astype(F32).reshape(PIECE, HALF)
            gs[side, rows] = both_ref[group, 1, :, :, lanes].astype(F32).reshape(PIECE, HALF)
    mask[...] = (
        lax.broadcasted_iota(jnp.int32, (LANES, HALF), 0) // MEMBERS
        == lax.broadcasted_iota(jnp.int32, (LANES, HALF), 1) // HEAD_DIM
    ).astype(F32).astype(B16)
    gain1 = gain1_ref[...]
    gain2 = gain2_ref[...]

    def patch_rows(ref, patch):
        return jnp.concatenate(
            [ref[side, pl.ds(patch, MEMBERS, stride=SPREAD), :] for side in range(2)], axis=1
        )

    def spread_heads(rows):
        return jnp.concatenate([rows] * HALF_HEADS, axis=0) * mask[...]

    inverse1, inverse2 = {}, {}
    gain_sums = [jnp.zeros((MEMBERS, WIDTH), F32), jnp.zeros((MEMBERS, WIDTH), F32)]
    rows_of = [slice(first, first + GROUP * MEMBERS) for first in range(0, TOKENS, GROUP * MEMBERS)]
    groups = [range(first, first + GROUP) for first in range(0, SPREAD, GROUP)]

    def part(ref, index, patch, side):
        return ref[blocks[patch], index * WIDTH + side * HALF : index * WIDTH + (side + 1) * HALF]

    def keep_grad(index, patch, side, grad):
        gqkv[blocks[patch], index * WIDTH + side * HALF : index * WIDTH + (side + 1) * HALF] = grad.astype(B16)

    def keep_part(first, total):
        rows = total.shape[0] // 2
        for half in range(2):
            parts[half, first : first + rows] = total[half * rows : (half + 1) * rows].astype(B16)

    def first_norm(group):
        for patch in groups[group]:
            rows = blocks[patch]
            unit, inverse1[patch] = norm_rows(patch_rows(xs, patch))
            unit1s[rows] = unit
            n1s[rows] = (unit * gain1).astype(B16)
            ogs[rows] = patch_rows(gs, patch).astype(B16)

    def project(group):
        rows = rows_of[group]
        for i in range(3):
            lanes = slice(i * WIDTH, (i + 1) * WIDTH)
            qkv[rows, lanes] = jnp.dot(n1s[rows], wqkv_ref[:, lanes], preferred_element_type=F32).astype(B16)

    def score(group):
        for patch in groups[group]:
            for side in range(2):
                spread_query = spread_heads(part(qkv, 0, patch, side))
                expanded[patch, side] = spread_query
                probs[patch, side] = dot(part(qkv, 1, patch, side), spread_query, (1, 1)) * SCALE

    def soften(group):
        for patch in groups[group]:
            for side in range(2):
                scores = probs[patch, side]
                scores = jnp.exp(scores - jnp.max(scores, axis=0, keepdims=True))
                weights = scores * (1.0 / jnp.sum(scores, axis=0, keepdims=True))
                probs[patch, side] = weights
                rounded[patch, side] = weights.astype(B16)

    def mix(group):
        for patch in groups[group]:
            for side in range(2):
                mixed = own_heads(dot(rounded[patch, side], part(qkv, 2, patch, side), (0, 0)))
                mixs[blocks[patch], halves[side]] = mixed.astype(B16)

    def join(group):
        rows = rows_of[group]
        products[rows] = jnp.dot(mixs[rows], wout_ref[...], preferred_element_type=F32)

    def second_norm(group):
        for patch in groups[group]:
            rows = blocks[patch]
            unit, inverse2[patch] = norm_rows(patch_rows(xs, patch) + products[rows])
            unit2s[rows] = unit
            n2s[rows] = (unit * gain2).astype(B16)

    def rise(group):
        rows = rows_of[group]
        for i in range(HIDDEN // WIDTH):
            lanes = slice(i * WIDTH, (i + 1) * WIDTH)
            wide_products[group % 2, 0, :, lanes] = jnp.dot(n2s[rows], wup_ref[:, lanes], preferred_element_type=F32)
            wide_products[group % 2, 1, :, lanes] = dot(ogs[rows], wdown_ref[lanes], (1, 1))

    def curve(group):
        for i in range(HIDDEN // WIDTH):
            lanes = slice(i * WIDTH, (i + 1) * WIDTH)
            for index, patch in enumerate(groups[group]):
                here = slice(index * MEMBERS, (index + 1) * MEMBERS)
                activated, slopes = gelu_pair(wide_products[group % 2, 0, here, lanes])
                acts[blocks[patch], lanes] = activated.astype(B16)
                gpre[blocks[patch], lanes] = (wide_products[group % 2, 1, here, lanes] * slopes).astype(B16)

    def fall(group):
        rows = rows_of[group]
        products[rows] = dot(gpre[rows], wup_ref[...], (1, 1))

    def second_back(group):
        for patch in groups[group]:
            rows = blocks[patch]
            unit, grad = unit2s[rows], products[rows]
            gain_sums[1] = gain_sums[1] + grad * unit
            back = norm_back(unit, inverse2[patch], gain2, grad)
            backs[rows] = back
            gas[rows] = (ogs[rows].astype(F32) + back).astype(B16)

    def part_back(group):
        rows = rows_of[group]
        gmix[rows] = dot(gas[rows], wout_ref[...], (1, 1)).astype(B16)

    def meet(group):
        for patch in groups[group]:
            for side in range(2):
                spread_grad = spread_heads(gmix[blocks[patch], halves[side]])
                dprobs[patch, side] = dot(part(qkv, 2, patch, side), spread_grad, (1, 1))
                keep_grad(2, patch, side, jnp.dot(rounded[patch, side], spread_grad, preferred_element_type=F32))

    def bend(group):
        for patch in groups[group]:
            for side in range(2):
                weights = probs[patch, side]
                product = weights * dprobs[patch, side]
                dscore = (product - weights * jnp.sum(product, axis=0, keepdims=True)) * SCALE
                rounded[patch, side] = dscore.astype(B16)

    def finish(group):
        for patch in groups[group]:
            for side in range(2):
                dscore = rounded[patch, side]
                keep_grad(1, patch, side, jnp.dot(dscore, expanded[patch, side], preferred_element_type=F32))
                keep_grad(0, patch, side, own_heads(dot(dscore, part(qkv, 1, patch, side), (0, 0))))

    def first_fall(group):
        rows = rows_of[group]
        products[rows] = dot(gqkv[rows], wqkv_ref[...], (1, 1))

    def first_back(group):
        for patch in groups[group]:
            rows = blocks[patch]
            unit, grad = unit1s[rows], products[rows]
            gain_sums[0] = gain_sums[0] + grad * unit
            delta = backs[rows] + norm_back(unit, inverse1[patch], gain1, grad)
            for side, lanes in enumerate(halves):
                ds[side, pl.ds(patch, MEMBERS, stride=SPREAD), :] = delta[:, lanes]

    def weigh(i):
        lanes = slice(i * WIDTH, (i + 1) * WIDTH)
        keep_part(4 * HALF + i * HALF, dot(n2s[...], gpre[:, lanes], (0, 0)))
        first = 8 * HALF + i % 2 * WIDTH
        parts[i // 2, first : first + WIDTH] = dot(ogs[...], acts[:, lanes], (0, 0)).T.astype(B16)

    stages = (
        first_norm, project, score, soften, mix, join, second_norm, rise, curve,
        fall, second_back, part_back, meet, bend, finish, first_fall, first_back,
    )
    weigh_from = len(groups) + stages.index(curve)
    for step in range(len(groups) + len(stages) - 1):
        for late, stage in enumerate(stages):
            if 0 <= step - late < len(groups):
                stage(step - late)
        if 0 <= step - weigh_from < HIDDEN // WIDTH:
            weigh(step - weigh_from)
    gain1_sum, gain2_sum = gain_sums

    part_qkv = dot(n1s[...], gqkv[...], (0, 0))
    for i in range(3):
        keep_part(i * HALF, part_qkv[:, i * WIDTH : (i + 1) * WIDTH])
    keep_part(3 * HALF, dot(mixs[...], gas[...], (0, 0)))
    gain_rows = jnp.concatenate(
        [jnp.sum(total, axis=0, keepdims=True) for total in (gain1_sum, gain2_sum)]
        + [jnp.zeros((GAIN_ROWS - 2, WIDTH), F32)],
        axis=0,
    ).astype(B16)
    for target, side in ((keep_ref, core), (give_ref, 1 - core)):
        for chip in range(CHIPS):
            target[chip, :ROWS] = parts[side, chip * ROWS : (chip + 1) * ROWS]
            target[chip, ROWS:CHUNK] = gain_rows
            start = pl.multiple_of((2 * chip + side) * PIECE, PIECE)
            for half, lanes in enumerate(halves):
                target[chip, CHUNK:, lanes] = ds[half, pl.ds(start, PIECE)].astype(B16)


def run_layer(core, both, gain1, wqkv, wout, gain2, wup, wdown):
    rows = (TOKENS, WIDTH)
    scratch = [
        pltpu.VMEM((2, TOKENS, HALF), F32),
        pltpu.VMEM((2, TOKENS, HALF), F32),
        pltpu.VMEM((2, TOKENS, HALF), F32),
        pltpu.VMEM((LANES, HALF), B16),
        pltpu.VMEM((TOKENS, 3 * WIDTH), B16),
        pltpu.VMEM((SPREAD, 2, LANES, HALF), B16),
        pltpu.VMEM((SPREAD, 2, MEMBERS, LANES), F32),
        pltpu.VMEM((SPREAD, 2, MEMBERS, LANES), F32),
        pltpu.VMEM((SPREAD, 2, MEMBERS, LANES), B16),
        pltpu.VMEM(rows, B16),
        pltpu.VMEM(rows, B16),
        pltpu.VMEM(rows, B16),
        pltpu.VMEM(rows, B16),
        pltpu.VMEM(rows, B16),
        pltpu.VMEM(rows, B16),
        pltpu.VMEM((TOKENS, 3 * WIDTH), B16),
        pltpu.VMEM((TOKENS, HIDDEN), B16),
        pltpu.VMEM((TOKENS, HIDDEN), B16),
        pltpu.VMEM(rows, F32),
        pltpu.VMEM(rows, F32),
        pltpu.VMEM(rows, F32),
        pltpu.VMEM(rows, F32),
        pltpu.VMEM((2, 2, GROUP * MEMBERS, HIDDEN), F32),
        pltpu.VMEM((2, CHIPS * ROWS, WIDTH), B16),
    ]
    shape = shaped(CHIPS, CHUNK + PIECE, WIDTH)
    return pl.pallas_call(
        layer_kernel,
        out_shape=(shape, shape),
        in_specs=[SMEM] + [VMEM] * 7,
        out_specs=(VMEM, VMEM),
        scratch_shapes=scratch,
        compiler_params=pltpu.CompilerParams(vmem_limit_bytes=48 * 1024 * 1024),
        cost_estimate=pl.CostEstimate(flops=5_000_000_000, bytes_accessed=6_000_000, transcendentals=2_000_000),
    )(core, both, gain1, wqkv, wout, gain2, wup, wdown)


def pack_kernel(input_ref, grad_ref, out_ref, held, in_sems, out_sems):
    pairs = []
    for own in range(OWN):
        for side, ref in enumerate((input_ref, grad_ref)):
            pairs.append(
                (
                    pltpu.make_async_copy(ref.at[own], held.at[side, own], in_sems.at[side, own]),
                    pltpu.make_async_copy(
                        held.at[side, own].reshape(GROUPS, SPREAD, WIDTH),
                        out_ref.at[:, side, own],
                        out_sems.at[side, own],
                    ),
                )
            )
    for arrive, _ in pairs:
        arrive.start()
    for arrive, leave in pairs:
        arrive.wait()
        leave.start()
    for _, leave in pairs:
        leave.wait()


def pack(layer_input, out_grad):
    return pl.pallas_call(
        pack_kernel,
        out_shape=shaped(GROUPS, 2, OWN, SPREAD, WIDTH),
        in_specs=[HBM, HBM],
        out_specs=HBM,
        scratch_shapes=[
            pltpu.VMEM((2, OWN, GROUPS * SPREAD, WIDTH), B16),
            pltpu.SemaphoreType.DMA((2, OWN)),
            pltpu.SemaphoreType.DMA((2, OWN)),
        ],
    )(layer_input, out_grad)


def pair_kernel(keep_ref, got_ref, out_ref):
    for chip in range(CHIPS):
        total = keep_ref[chip, :CHUNK].astype(F32) + got_ref[chip, :CHUNK].astype(F32)
        out_ref[chip, :CHUNK] = total.astype(B16)
        out_ref[chip, CHUNK : CHUNK + PIECE] = keep_ref[chip, CHUNK:]
        out_ref[chip, CHUNK + PIECE :] = got_ref[chip, CHUNK:]


def sum_kernel(got_ref, out_ref):
    total = got_ref[0, :CHUNK].astype(F32)
    for chip in range(1, CHIPS):
        total = total + got_ref[chip, :CHUNK].astype(F32)
    out_ref[...] = total.astype(B16)


def four(refs):
    own, first, second, third = (ref[...].astype(F32) for ref in refs)
    return ((own + first) + (second + third)).astype(B16)


def round_kernel(own_ref, first_ref, second_ref, third_ref, out_ref):
    out_ref[...] = four((own_ref, first_ref, second_ref, third_ref))


def last_round_kernel(own_ref, first_ref, second_ref, third_ref, done_ref, out_ref, gains_ref):
    del done_ref
    total = four((own_ref, first_ref, second_ref, third_ref))
    for chip in range(CHIPS):
        out_ref[chip] = total[:ROWS]
    gains_ref[...] = total[ROWS:]


def home_kernel(core_ref, got_ref, grad_ref, out_ref, done_ref):
    done_ref[...] = jnp.zeros_like(done_ref)
    core = core_ref[0]
    for chip in range(CHIPS):
        for part in range(2):
            index = 2 * chip + (core if part == 0 else 1 - core)
            there = pl.ds(pl.multiple_of(index * SPREAD, SPREAD), SPREAD)
            first = CHUNK + part * PIECE
            for own in range(OWN):
                moved = got_ref[chip, first + own * SPREAD : first + (own + 1) * SPREAD]
                out_ref[own, there] = grad_ref[own, there].astype(F32) + moved.astype(F32)


def write_half(scale, side, part_ref, out_refs, held, held_up, sems):
    copies = []

    def send(source, out_ref, rows, index):
        there = pl.ds(pl.multiple_of(side * rows, rows), rows)
        copies.append(pltpu.make_async_copy(source, out_ref.at[there], sems.at[index]))
        copies[-1].start()

    for index in range(4):
        rows = slice(index * HALF, (index + 1) * HALF)
        held[rows] = part_ref[rows].astype(F32) * scale
        send(held.at[rows], out_refs[index], HALF, index)
    for index in range(HIDDEN // WIDTH):
        first = (4 + index) * HALF
        held_up[:, index * WIDTH : (index + 1) * WIDTH] = part_ref[first : first + HALF].astype(F32) * scale
    send(held_up, out_refs[4], HALF, 4)
    rows = slice(8 * HALF, 12 * HALF)
    held[rows] = part_ref[rows].astype(F32) * scale
    send(held.at[rows], out_refs[5], 4 * HALF, 5)
    for copy in copies:
        copy.wait()


def mine_kernel(scale, core_ref, part_ref, gains_ref, *refs):
    refs[6][...] = gains_ref[0:1].astype(F32) * scale
    refs[7][...] = gains_ref[1:2].astype(F32) * scale
    write_half(scale, core_ref[0], part_ref, refs[:6], *refs[8:])


def theirs_kernel(scale, core_ref, part_ref, *refs):
    write_half(scale, 1 - core_ref[0], part_ref, refs[6:12], *refs[12:])


FINAL_SCRATCH = (
    pltpu.VMEM((CHIPS * ROWS, WIDTH), F32),
    pltpu.VMEM((HALF, HIDDEN), F32),
    pltpu.SemaphoreType.DMA((6,)),
)


def local(kernel, out_shape, specs, *operands):
    return pl.pallas_call(
        kernel,
        out_shape=out_shape,
        in_specs=specs,
        out_specs=jax.tree.map(lambda _: VMEM, out_shape),
        compiler_params=pltpu.CompilerParams(vmem_limit_bytes=32 * 1024 * 1024),
    )(*operands)


def shaped(*shape, dtype=B16):
    return jax.ShapeDtypeStruct(shape, dtype)


def swap(array, axis, groups=None):
    return lax.all_to_all(
        array, axis, split_axis=0, concat_axis=0, tiled=True, axis_index_groups=groups
    )


def on_device(
    layer_input, out_grad, norm1_gain, w_query, w_key, w_value, w_out, norm2_gain, w_up, w_down
):
    members = lax.axis_size("member")
    spaces = lax.axis_size("space")
    core = (lax.axis_index("member") % 2).astype(jnp.int32).reshape(1)
    other_core = [(k, k ^ 1) for k in range(members)]
    same_core = [[c + 2 * k for k in range(CHIPS)] for c in range(2)]

    def across(array, steps):
        return [lax.ppermute(array, "space", [(k, k ^ step) for k in range(spaces)]) for step in steps]

    both = swap(pack(layer_input, out_grad), "member")
    wqkv = jnp.concatenate([w_query, w_key, w_value], axis=1)
    keep, give = run_layer(
        core, both, norm1_gain.reshape(1, WIDTH), wqkv, w_out, norm2_gain.reshape(1, WIDTH), w_up, w_down
    )
    got = lax.ppermute(give, "member", other_core)
    sent = local(pair_kernel, shaped(CHIPS, CHUNK + 2 * PIECE, WIDTH), [VMEM] * 2, keep, got)
    got = swap(sent, "member", same_core)
    input_grad, done = local(
        home_kernel,
        (shaped(OWN, GROUPS * SPREAD, WIDTH, dtype=F32), shaped(8, HALF, dtype=F32)),
        [SMEM, VMEM, VMEM],
        core,
        got,
        out_grad,
    )
    chunk = shaped(CHUNK, WIDTH)
    total = local(sum_kernel, chunk, [VMEM], got)
    total = local(round_kernel, chunk, [VMEM] * 4, total, *across(total, (2, 4, 6) ))
    sent, gains = local(
        last_round_kernel,
        (shaped(CHIPS, ROWS, WIDTH), shaped(GAIN_ROWS, WIDTH)),
        [VMEM] * 5,
        total,
        *across(total, (1, 8, 9)),
        done,
    )
    mine = swap(sent, "member", same_core).reshape(CHIPS * ROWS, WIDTH)
    theirs = lax.ppermute(mine, "member", other_core)
    scale = 1.0 / math.sqrt(MEMBERS * GROUPS * SPREAD * spaces)
    square = shaped(WIDTH, WIDTH, dtype=F32)
    row = shaped(1, WIDTH, dtype=F32)
    grads_shape = (square, square, square, square, shaped(WIDTH, HIDDEN, dtype=F32), shaped(HIDDEN, WIDTH, dtype=F32))
    params = pltpu.CompilerParams(vmem_limit_bytes=32 * 1024 * 1024)
    *grads, gain1, gain2 = pl.pallas_call(
        functools.partial(mine_kernel, scale),
        out_shape=(*grads_shape, row, row),
        in_specs=[SMEM, VMEM, VMEM],
        out_specs=(*[HBM] * 6, VMEM, VMEM),
        scratch_shapes=FINAL_SCRATCH,
        compiler_params=params,
    )(core, mine, gains)
    grads = pl.pallas_call(
        functools.partial(theirs_kernel, scale),
        out_shape=grads_shape,
        in_specs=[SMEM, VMEM, *[HBM] * 6],
        out_specs=(HBM,) * 6,
        input_output_aliases={2 + index: index for index in range(6)},
        scratch_shapes=FINAL_SCRATCH,
        compiler_params=params,
    )(core, theirs, *grads)
    return (input_grad, *grads, gain1.reshape(WIDTH), gain2.reshape(WIDTH))


def solution(mesh):
    in_specs = (
        P("member", "space", None),
        P("member", "space", None),
        P(),
        P(),
        P(),
        P(),
        P(),
        P(),
        P(),
        P(),
    )
    out_specs = (P("member", "space", None), P(), P(), P(), P(), P(), P(), P(), P())
    return jax.shard_map(
        on_device, mesh=mesh, in_specs=in_specs, out_specs=out_specs, check_vma=False
    )
```
